512 devices in a mesh: row: 32 (over z, core), col: 16 (over x, y).
Axes of the slice: x: 4, y: 4, z: 16, core: 2. Of those that a mesh axis runs over, the one named last changes fastest.
Arguments:
- inputs: bfloat16 [256, 12288], P('col', 'row'), may hold values from -6 to 6
- w_in: bfloat16 [12288, 24576], P('row', 'col'), may hold values from -0.0546875 to 0.0546875
- w_out: bfloat16 [24576, 12288], P('col', 'row'), may hold values from -0.0390625 to 0.0390625
- cotangent: bfloat16 [256, 12288], P('col', 'row'), may hold values from -1.5 to 1.5
Outputs:
- output: bfloat16 [256, 12288], P('col', 'row')
- input_grad: bfloat16 [256, 12288], P('col', 'row')
- w_in_grad: bfloat16 [12288, 24576], P('row', 'col')
- w_out_grad: bfloat16 [24576, 12288], P('col', 'row')
The draws below stay inside these ranges and needn't reach their ends.
All inputs are finite; a program needn't handle non-finite values.
Results may differ from the reference program's by a relative error of at most 0.005.
Values may be sent and summed in bfloat16 or wider, within the bound.
A program may use at most 64 MiB of HBM per device.

```python
import jax
import jax.numpy as jnp

D = 12288
FF = 24576
TOKENS = 256


def raised(values, rng, source, target, blocks, factor):
    owner, partner = [(jnp.arange(values.shape[axis_at]) // (values.shape[axis_at] // blocks)).reshape([-1 if axis == axis_at else 1 for axis in range(values.ndim)]) for axis_at in (source, target)]
    chosen = jax.random.permutation(rng, blocks)[partner]
    strong = (owner == chosen) | (owner == (partner + blocks // 2) % blocks)
    return jnp.where(strong, factor * values, values)


def steps_of(stream_key, extent, split, low, largest):
    def one(axis_at, parts):
        heights = jax.random.uniform(jax.random.fold_in(jax.random.fold_in(stream_key, 6), axis_at), (parts,), jnp.float32, low / len(split), largest / len(split))
        return jnp.repeat(jnp.exp(heights), extent[axis_at] // parts).reshape((-1,) + (1,) * (len(extent) - axis_at - 1))

    factor_of = one(*split[0])
    for cut in split[1:]:
        factor_of = factor_of * one(*cut)
    return factor_of


def centred(stream_key, dims, spread, reach, pieces=(), dtype=jnp.bfloat16):
    array = spread * jax.random.normal(stream_key, dims, jnp.float32)
    if pieces:
        array = array * steps_of(stream_key, dims, pieces, -0.22, 0.18)
    return jnp.clip(array, -reach, reach).astype(dtype)


def noise_with(own_key, extent, spread, limit, pieces, heavy, dtype=jnp.bfloat16):
    result = spread * jax.random.normal(own_key, extent, jnp.float32)
    if pieces:
        result = result * steps_of(own_key, extent, pieces, -0.22, 0.18)
    return jnp.clip(raised(result, jax.random.fold_in(own_key, 3), *heavy), -limit, limit).astype(dtype)


def setup_inputs(seed: int = 0) -> dict:
    key_of = jax.random.split(jax.random.key(seed), 5)
    return {
        "inputs": noise_with(key_of[0], (TOKENS, D), 1.0, 6.0, ((0, 16), (1, 32)), (1, 0, 32, 2.75)),
        "w_in": centred(key_of[1], (D, FF), D ** -0.5, 0.0546875, ((0, 32), (1, 16))),
        "w_out": centred(key_of[2], (FF, D), FF ** -0.5, 0.0390625, ((0, 16), (1, 32))),
        "cotangent": noise_with(key_of[3], (TOKENS, D), 0.25, 1.5, ((0, 16), (1, 32)), (1, 0, 32, 2.75)),
    }


gelu_coef = 0.7978845608
cubic_coef = 0.044715


def gelu_tanh(value):
    return 0.5 * value * (1.0 + jnp.tanh(gelu_coef * (value + cubic_coef * value * value * value)))


def gelu_slope(value):
    inner = jnp.tanh(gelu_coef * (value + cubic_coef * value * value * value))
    return 0.5 * (1.0 + inner) + 0.5 * value * (1.0 - inner * inner) * gelu_coef * (1.0 + 3.0 * cubic_coef * value * value)


def reference(inputs, w_in, w_out, cotangent):
    pre_act = jnp.dot(inputs, w_in, preferred_element_type=jnp.float32)
    hidden = gelu_tanh(pre_act).astype(jnp.bfloat16)
    output = jnp.dot(hidden, w_out, preferred_element_type=jnp.float32).astype(jnp.bfloat16)
    w_out_grad = jnp.dot(hidden.T, cotangent, preferred_element_type=jnp.float32).astype(jnp.bfloat16)
    hidden_grad = jnp.dot(cotangent, w_out.T, preferred_element_type=jnp.float32)
    pre_grad = (hidden_grad * gelu_slope(pre_act)).astype(jnp.bfloat16)
    w_in_grad = jnp.dot(inputs.T, pre_grad, preferred_element_type=jnp.float32).astype(jnp.bfloat16)
    input_grad = jnp.dot(pre_grad, w_in.T, preferred_element_type=jnp.float32).astype(jnp.bfloat16)
    return output, input_grad, w_in_grad, w_out_grad
```

```python
import jax
import jax.numpy as jnp
from jax import lax
from jax.experimental import pallas as pl
from jax.experimental.pallas import tpu as pltpu
from jax.sharding import PartitionSpec as P

MESH = pl.DeviceIdType.MESH
gelu_coef = 0.7978845608
cubic_coef = 0.044715

CHIPS = 16
COLS = 16
BLOCK = 16
TOKENS = 256
DEPTH = 384
UNITS = 1536
HALF = 768

PARENT = {
    3: 0, -3: 0, 1: 0, -1: 0, 6: 3, -6: -3, 4: 3, -4: -3, 2: 1, -2: -1, 8: 6, 7: 6, -7: -6, 5: 4, -5: -4,
}
CHILDREN = {}
for child, parent in PARENT.items():
    CHILDREN.setdefault(parent, []).append(child)
FAR_FIRST = (
    (2, 2), (1, 2), (3, 2), (2, 1), (2, 3), (0, 2), (2, 0), (1, 1), (1, 3), (3, 1), (3, 3), (0, 1), (0, 3), (1, 0), (3, 0),
)
FIRST = (8, 7, -7, 5, -5, 2, -2)
SECOND = (6, -6, 4, -4, 1, -1)
THIRD = (3, -3)
OFFSETS = sorted({PARENT[r] - r for r in PARENT} | {r - PARENT[r] for r in PARENT})
MIDDLE, LOW, HIGH = range(4, 12), range(0, 4), range(12, 16)


def rows(role):
    return pl.ds((role + 7) * BLOCK, BLOCK)


def contract_last(left, right):
    return lax.dot_general(
        left, right, (((1,), (1,)), ((), ())), preferred_element_type=jnp.float32
    )


def contract_first(left, right):
    return lax.dot_general(
        left, right, (((0,), (0,)), ((), ())), preferred_element_type=jnp.float32
    )


def kernel(
    inputs, w_in, w_out, cotangent,
    output, input_grad, w_in_grad, w_out_grad,
    tokens, tokens_twin, w_in_v, w_out_v, w_in_twin, w_out_twin, mine, sums, sums_in, units, send_out, recv_out,
    load_sem, own_sem, gather_send, gather_recv, pair_send, pair_recv, swap_send, swap_recv, sum_send, sum_recv,
    unit_send, unit_recv, twin_send, twin_recv, out_send, out_recv,
):
    row, col = lax.axis_index("row"), lax.axis_index("col")
    z, c = row // 2, lax.rem(row, 2)
    twin = (z * 2 + 1 - c, col)

    def along(offset):
        return (lax.rem(z + offset + CHIPS, CHIPS) * 2 + c, col)

    def across(step):
        return (row, lax.rem(col // 4 + step[0], 4) * 4 + lax.rem(lax.rem(col, 4) + step[1], 4))

    def send(src, dst, send_sem, recv_sem, device):
        pltpu.make_async_remote_copy(
            src_ref=src, dst_ref=dst, send_sem=send_sem, recv_sem=recv_sem,
            device_id=device, device_id_type=MESH,
        ).start()

    def wait(ref, sem):
        pltpu.make_async_copy(ref, ref, sem).wait()

    here = pl.ds(pl.multiple_of(lax.rem(z - col + 7 + CHIPS, CHIPS) * BLOCK, BLOCK), BLOCK)

    own = [
        pltpu.make_async_copy(source, tokens.at[k, here], own_sem.at[k])
        for k, source in enumerate((inputs, cotangent))
    ]
    loads = [
        pltpu.make_async_copy(w_in.at[:, pl.ds(h * HALF, HALF)], w_in_v.at[h], load_sem.at[h])
        for h in range(2)
    ] + [pltpu.make_async_copy(w_out.at[pl.ds(h * HALF, HALF)], w_out_v.at[h], load_sem.at[2 + h]) for h in range(2)]
    for copy in own + loads:
        copy.start()

    barrier = pltpu.get_barrier_semaphore()
    peers = [across(step) for step in FAR_FIRST] + [along(offset) for offset in OFFSETS] + [twin]
    for peer in peers:
        pl.semaphore_signal(barrier, inc=1, device_id=peer, device_id_type=MESH)
    pl.semaphore_wait(barrier, len(peers))

    for k in range(2):
        own[k].wait()
        for step in FAR_FIRST:
            send(tokens.at[k, here], tokens.at[k, here], gather_send.at[k], gather_recv.at[k], across(step))
        if k == 0:
            theirs = w_in.at[:, pl.ds(pl.multiple_of((1 - c) * HALF, HALF), HALF)]
            send(theirs, w_in_twin, swap_send.at[0], swap_recv.at[0], twin)
        else:
            theirs = w_out.at[pl.ds(pl.multiple_of((1 - c) * HALF, HALF), HALF)]
            send(theirs, w_out_twin, swap_send.at[1], swap_recv.at[1], twin)
    for copy in loads:
        copy.wait()

    def first_round(k):
        wait(tokens.at[k, pl.ds(0, (COLS - 1) * BLOCK)], gather_recv.at[k])
        send(tokens.at[k], tokens_twin.at[k], pair_send.at[k], pair_recv.at[k], twin)
        if k == 0:
            mine[0] = jnp.dot(tokens[0], w_in_v[c], preferred_element_type=jnp.float32)
            wait(w_in_twin, swap_recv.at[0])
            wait(tokens_twin.at[0], pair_recv.at[0])
            mine[0] += jnp.dot(tokens_twin[0], w_in_twin[...], preferred_element_type=jnp.float32)
        else:
            mine[1] = contract_last(tokens[1], w_out_v[c])
            wait(w_out_twin, swap_recv.at[1])
            wait(tokens_twin.at[1], pair_recv.at[1])
            mine[1] += contract_last(tokens_twin[1], w_out_twin[...])
        for role in FIRST:
            pass_on(k, role)

    def collected(k, role):
        value = mine[k, rows(role)]
        for child in CHILDREN.get(role, ()):
            wait(sums_in.at[k, rows(child)], sum_recv.at[k, child + 7])
            value = value + sums_in[k, rows(child)].astype(jnp.float32)
        return value

    def pass_on(k, role):
        sums[k, rows(role)] = collected(k, role).astype(jnp.bfloat16)
        send(
            sums.at[k, rows(role)], sums_in.at[k, rows(role)], sum_send.at[k], sum_recv.at[k, role + 7],
            along(PARENT[role] - role),
        )

    def hand_out(k, role):
        for child in CHILDREN.get(role, ()):
            send(
                units.at[k, c, rows(role)], units.at[k, c, rows(child)], unit_send.at[k], unit_recv.at[k, child + 7],
                along(child - role),
            )
        group = 0 if role + 7 in MIDDLE else 1 if role + 7 in LOW else 2
        send(units.at[k, c, rows(role)], units.at[k, c, rows(role)], twin_send.at[k], twin_recv.at[k, group], twin)

    def relay(k, role):
        wait(units.at[k, c, rows(role)], unit_recv.at[k, role + 7])
        hand_out(k, role)

    def unit_terms(k, group, blocks):
        span = pl.ds(blocks[0] * BLOCK, len(blocks) * BLOCK)
        wait(units.at[k, 1 - c, span], twin_recv.at[k, group])
        if k == 0:
            value = jnp.dot(units[0, 0, span], w_out_v[0], preferred_element_type=jnp.float32)
            value = value + jnp.dot(units[0, 1, span], w_out_v[1], preferred_element_type=jnp.float32)
        else:
            value = contract_last(units[1, 0, span], w_in_v[0])
            value = value + contract_last(units[1, 1, span], w_in_v[1])
        send_out[k, span] = value.astype(jnp.bfloat16)
        for p in blocks:
            target = lax.rem(z + 7 - p + CHIPS, CHIPS)
            source = send_out.at[k, pl.ds(p * BLOCK, BLOCK)]

            @pl.when(target != col)
            def _():
                send(source, recv_out.at[k, col], out_send.at[k], out_recv.at[k], (row, target))

            @pl.when(target == col)
            def _():
                recv_out[k, col] = source[...]

    first_round(0)
    first_round(1)
    for k in range(2):
        for role in SECOND:
            pass_on(k, role)
    for k in range(2):
        for role in THIRD:
            pass_on(k, role)

    pre_act = collected(0, 0)
    inner = jnp.tanh(gelu_coef * (pre_act + cubic_coef * pre_act * pre_act * pre_act))
    units[0, c, rows(0)] = (0.5 * pre_act * (1.0 + inner)).astype(jnp.bfloat16)
    hand_out(0, 0)
    slope = 0.5 * (1.0 + inner) + 0.5 * pre_act * (1.0 - inner * inner) * gelu_coef * (
        1.0 + 3.0 * cubic_coef * pre_act * pre_act
    )
    units[1, c, rows(0)] = (collected(1, 0) * slope).astype(jnp.bfloat16)
    hand_out(1, 0)

    for group in (THIRD + (1, -1), (6, -6, 4, -4, 2, -2)):
        for k in range(2):
            for role in group:
                relay(k, role)
    for k in range(2):
        unit_terms(k, 0, MIDDLE)
        for role in (8, 7, -7, 5, -5):
            relay(k, role)
    for k in range(2):
        unit_terms(k, 1, LOW)
        unit_terms(k, 2, HIGH)
    for h in range(2):
        span = pl.ds(h * HALF, HALF)
        w_out_grad[span, :] = contract_first(units[0, h], tokens[1]).astype(jnp.bfloat16)
        w_in_grad[:, span] = contract_first(tokens[0], units[1, h]).astype(jnp.bfloat16)
    for k in range(2):
        wait(recv_out.at[k, pl.ds(0, COLS - 1)], out_recv.at[k])
        value = recv_out[k, 0].astype(jnp.float32)
        for source in range(1, COLS):
            value = value + recv_out[k, source].astype(jnp.float32)
        (output, input_grad)[k][...] = value.astype(jnp.bfloat16)

    for k in range(2):
        span = pl.ds(0, (COLS - 1) * BLOCK)
        wait(tokens.at[k, span], gather_send.at[k])
        wait(tokens_twin.at[k], pair_send.at[k])
        wait(sums.at[k, span], sum_send.at[k])
        wait(units.at[k, 0, span], unit_send.at[k])
        wait(units.at[k, 0], twin_send.at[k])
        wait(send_out.at[k, span], out_send.at[k])
    wait(w_in_twin, swap_send.at[0])
    wait(w_out_twin, swap_send.at[1])


def place(*refs):
    copies = [pltpu.make_async_copy(refs[i], refs[4 + i], refs[8].at[i]) for i in range(4)]
    for copy in copies:
        copy.start()
    for copy in copies:
        copy.wait()


def exchange(inputs, w_in, w_out, cotangent):
    bf16, f32 = jnp.bfloat16, jnp.float32
    dma = pltpu.SemaphoreType.DMA
    hbm, vmem = pl.BlockSpec(memory_space=pltpu.HBM), pl.BlockSpec(memory_space=pltpu.VMEM)
    shape = jax.ShapeDtypeStruct
    return pl.pallas_call(
        kernel,
        out_shape=(
            shape((BLOCK, DEPTH), bf16),
            shape((BLOCK, DEPTH), bf16),
            shape((DEPTH, UNITS), bf16),
            shape((UNITS, DEPTH), bf16),
        ),
        in_specs=[hbm] * 4,
        out_specs=(vmem,) * 4,
        scratch_shapes=[
            pltpu.VMEM((2, TOKENS, DEPTH), bf16),
            pltpu.VMEM((2, TOKENS, DEPTH), bf16),
            pltpu.VMEM((2, DEPTH, HALF), bf16),
            pltpu.VMEM((2, HALF, DEPTH), bf16),
            pltpu.VMEM((DEPTH, HALF), bf16),
            pltpu.VMEM((HALF, DEPTH), bf16),
            pltpu.VMEM((2, TOKENS, HALF), f32),
            pltpu.VMEM((2, TOKENS, HALF), bf16),
            pltpu.VMEM((2, TOKENS, HALF), bf16),
            pltpu.VMEM((2, 2, TOKENS, HALF), bf16),
            pltpu.VMEM((2, TOKENS, DEPTH), bf16),
            pltpu.VMEM((2, COLS, BLOCK, DEPTH), bf16),
            dma((4,)), dma((2,)), dma((2,)), dma((2,)), dma((2,)), dma((2,)), dma((2,)), dma((2,)),
            dma((2,)), dma((2, 16)), dma((2,)), dma((2, 16)), dma((2,)), dma((2, 3)), dma((2,)), dma((2,)),
        ],
        compiler_params=pltpu.CompilerParams(
            collective_id=0, has_side_effects=True, vmem_limit_bytes=40 * 1024 * 1024
        ),
        name="feed_forward",
    )(inputs, w_in, w_out, cotangent)


def local(inputs, w_in, w_out, cotangent):
    results = exchange(inputs, w_in, w_out, cotangent)
    return pl.pallas_call(
        place,
        out_shape=tuple(jax.ShapeDtypeStruct(result.shape, result.dtype) for result in results),
        in_specs=[pl.BlockSpec(memory_space=pltpu.VMEM)] * 4,
        out_specs=(pl.BlockSpec(memory_space=pltpu.HBM),) * 4,
        scratch_shapes=[pltpu.SemaphoreType.DMA((4,))],
        name="place",
    )(*results)


def solution(mesh):
    placed = (P("col", "row"), P("row", "col"), P("col", "row"), P("col", "row"))
    return jax.shard_map(
        local,
        mesh=mesh,
        in_specs=placed,
        out_specs=(P("col", "row"), P("col", "row"), P("row", "col"), P("col", "row")),
        check_vma=False,
    )
```

```python
import jax
import jax.numpy as jnp
from jax import lax
from jax.experimental import pallas as pl
from jax.experimental.pallas import tpu as pltpu
from jax.sharding import PartitionSpec as P

MESH = pl.DeviceIdType.MESH
gelu_coef = 0.7978845608
cubic_coef = 0.044715

CHIPS = 16
COLS = 16
BLOCK = 16
TOKENS = 256
DEPTH = 384
UNITS = 1536
HALF = 768
PIECES = 4
VMEM_LIMIT = 58 * 1024 * 1024

SUM_PARENT = {
    3: 0, -3: 0, 1: 0, -1: 0, 6: 3, -6: -3, 4: 3, -4: -3, 2: 1, -2: -1, 8: 6, 7: 6, -7: -6, 5: 4, -5: -4,
}
UNIT_PARENT = SUM_PARENT


def children_of(parents):
    children = {}
    for child, parent in parents.items():
        children.setdefault(parent, []).append(child)
    return children


SUM_CHILDREN, UNIT_CHILDREN = children_of(SUM_PARENT), children_of(UNIT_PARENT)


def height(role):
    return 1 + max((height(child) for child in SUM_CHILDREN.get(role, ())), default=-1)


def depth(role):
    return 1 + depth(UNIT_PARENT[role]) if role else 0


def levels(rank, parents):
    found = {}
    for role in sorted(parents, key=lambda role: -abs(role)):
        found.setdefault(rank(role), []).append(role)
    return [found[level] for level in sorted(found)]


SUM_LEVELS, UNIT_LEVELS = levels(height, SUM_PARENT), levels(depth, UNIT_PARENT)
FAR_FIRST = (
    (2, 2), (1, 2), (3, 2), (2, 1), (2, 3), (0, 2), (2, 0), (1, 1), (1, 3), (3, 1), (3, 3), (0, 1), (0, 3), (1, 0), (3, 0),
)
OFFSETS = sorted({way * (tree[r] - r) for tree in (SUM_PARENT, UNIT_PARENT) for r in tree for way in (1, -1)})
MIDDLE, LOW, HIGH = range(4, 12), range(0, 4), range(12, 16)


def rows(role):
    return pl.ds((role + 7) * BLOCK, BLOCK)


def contract_last(left, right):
    return lax.dot_general(
        left, right, (((1,), (1,)), ((), ())), preferred_element_type=jnp.float32
    )


def contract_first(left, right):
    return lax.dot_general(
        left, right, (((0,), (0,)), ((), ())), preferred_element_type=jnp.float32
    )


def kernel(
    inputs, w_in, w_out, cotangent,
    output, input_grad, w_in_grad, w_out_grad,
    tokens, tokens_twin, w_in_v, w_out_v, w_in_twin, w_out_twin, mine, sums, sums_in, units, send_out, recv_out,
    grad_in, grad_out, result, store_sem,
    load_sem, own_sem, gather_send, gather_recv, pair_send, pair_recv, swap_send, swap_recv, sum_send, sum_recv,
    unit_send, unit_recv, twin_send, twin_recv, out_send, out_recv,
):
    row, col = lax.axis_index("row"), lax.axis_index("col")
    z, c = row // 2, lax.rem(row, 2)
    twin = (z * 2 + 1 - c, col)

    def along(offset):
        return (lax.rem(z + offset + CHIPS, CHIPS) * 2 + c, col)

    def across(step):
        return (row, lax.rem(col // 4 + step[0], 4) * 4 + lax.rem(lax.rem(col, 4) + step[1], 4))

    def send(src, dst, send_sem, recv_sem, device):
        pltpu.make_async_remote_copy(
            src_ref=src, dst_ref=dst, send_sem=send_sem, recv_sem=recv_sem,
            device_id=device, device_id_type=MESH,
        ).start()

    def wait(ref, sem):
        pltpu.make_async_copy(ref, ref, sem).wait()

    here = pl.ds(pl.multiple_of(lax.rem(z - col + 7 + CHIPS, CHIPS) * BLOCK, BLOCK), BLOCK)

    own = [
        pltpu.make_async_copy(source, tokens.at[k, here], own_sem.at[k])
        for k, source in enumerate((inputs, cotangent))
    ]
    loads = [
        pltpu.make_async_copy(w_in.at[:, pl.ds(h * HALF, HALF)], w_in_v.at[h], load_sem.at[h])
        for h in range(2)
    ] + [pltpu.make_async_copy(w_out.at[pl.ds(h * HALF, HALF)], w_out_v.at[h], load_sem.at[2 + h]) for h in range(2)]
    for copy in own + loads:
        copy.start()

    barrier = pltpu.get_barrier_semaphore()
    peers = [across(step) for step in FAR_FIRST] + [along(offset) for offset in OFFSETS] + [twin]
    for peer in peers:
        pl.semaphore_signal(barrier, inc=1, device_id=peer, device_id_type=MESH)
    pl.semaphore_wait(barrier, len(peers))

    for k in range(2):
        own[k].wait()
        for step in FAR_FIRST:
            send(tokens.at[k, here], tokens.at[k, here], gather_send.at[k], gather_recv.at[k], across(step))
        if k == 0:
            theirs = w_in.at[:, pl.ds(pl.multiple_of((1 - c) * HALF, HALF), HALF)]
            send(theirs, w_in_twin, swap_send.at[0], swap_recv.at[0], twin)
        else:
            theirs = w_out.at[pl.ds(pl.multiple_of((1 - c) * HALF, HALF), HALF)]
            send(theirs, w_out_twin, swap_send.at[1], swap_recv.at[1], twin)
    for copy in loads:
        copy.wait()

    def first_round(k):
        wait(tokens.at[k, pl.ds(0, (COLS - 1) * BLOCK)], gather_recv.at[k])
        send(tokens.at[k], tokens_twin.at[k], pair_send.at[k], pair_recv.at[k], twin)
        if k == 0:
            mine[0] = jnp.dot(tokens[0], w_in_v[c], preferred_element_type=jnp.float32)
            wait(w_in_twin, swap_recv.at[0])
            wait(tokens_twin.at[0], pair_recv.at[0])
            mine[0] += jnp.dot(tokens_twin[0], w_in_twin[...], preferred_element_type=jnp.float32)
        else:
            mine[1] = contract_last(tokens[1], w_out_v[c])
            wait(w_out_twin, swap_recv.at[1])
            wait(tokens_twin.at[1], pair_recv.at[1])
            mine[1] += contract_last(tokens_twin[1], w_out_twin[...])
        for role in SUM_LEVELS[0]:
            pass_on(k, role)

    def collected(k, role):
        value = mine[k, rows(role)]
        for child in SUM_CHILDREN.get(role, ()):
            wait(sums_in.at[k, rows(child)], sum_recv.at[k, child + 7])
            value = value + sums_in[k, rows(child)].astype(jnp.float32)
        return value

    def pass_on(k, role):
        sums[k, rows(role)] = collected(k, role).astype(jnp.bfloat16)
        send(
            sums.at[k, rows(role)], sums_in.at[k, rows(role)], sum_send.at[k], sum_recv.at[k, role + 7],
            along(SUM_PARENT[role] - role),
        )

    def hand_out(k, role):
        for child in UNIT_CHILDREN.get(role, ()):
            send(
                units.at[k, c, rows(role)], units.at[k, c, rows(child)], unit_send.at[k], unit_recv.at[k, child + 7],
                along(child - role),
            )
        group = 0 if role + 7 in MIDDLE else 1 if role + 7 in LOW else 2
        send(units.at[k, c, rows(role)], units.at[k, c, rows(role)], twin_send.at[k], twin_recv.at[k, group], twin)

    def relay(k, role):
        wait(units.at[k, c, rows(role)], unit_recv.at[k, role + 7])
        hand_out(k, role)

    def unit_terms(k, group, blocks):
        span = pl.ds(blocks[0] * BLOCK, len(blocks) * BLOCK)
        wait(units.at[k, 1 - c, span], twin_recv.at[k, group])
        if k == 0:
            value = jnp.dot(units[0, 0, span], w_out_v[0], preferred_element_type=jnp.float32)
            value = value + jnp.dot(units[0, 1, span], w_out_v[1], preferred_element_type=jnp.float32)
        else:
            value = contract_last(units[1, 0, span], w_in_v[0])
            value = value + contract_last(units[1, 1, span], w_in_v[1])
        send_out[k, span] = value.astype(jnp.bfloat16)
        for p in blocks:
            target = lax.rem(z + 7 - p + CHIPS, CHIPS)
            source = send_out.at[k, pl.ds(p * BLOCK, BLOCK)]

            @pl.when(target != col)
            def _():
                send(source, recv_out.at[k, col], out_send.at[k], out_recv.at[k], (row, target))

            @pl.when(target == col)
            def _():
                recv_out[k, col] = source[...]

    first_round(0)
    first_round(1)
    for level in SUM_LEVELS[1:]:
        for k in range(2):
            for role in level:
                pass_on(k, role)

    pre_act = collected(0, 0)
    inner = jnp.tanh(gelu_coef * (pre_act + cubic_coef * pre_act * pre_act * pre_act))
    units[0, c, rows(0)] = (0.5 * pre_act * (1.0 + inner)).astype(jnp.bfloat16)
    hand_out(0, 0)
    slope = 0.5 * (1.0 + inner) + 0.5 * pre_act * (1.0 - inner * inner) * gelu_coef * (
        1.0 + 3.0 * cubic_coef * pre_act * pre_act
    )
    units[1, c, rows(0)] = (collected(1, 0) * slope).astype(jnp.bfloat16)
    hand_out(1, 0)

    for level in UNIT_LEVELS[:-1]:
        for k in range(2):
            for role in level:
                relay(k, role)
    for k in range(2):
        unit_terms(k, 0, MIDDLE)
        for role in UNIT_LEVELS[-1]:
            relay(k, role)
    for k in range(2):
        unit_terms(k, 1, LOW)
        unit_terms(k, 2, HIGH)
    stores = []
    for h in range(2):
        span = pl.ds(h * HALF, HALF)
        grad_out[h] = contract_first(units[0, h], tokens[1]).astype(jnp.bfloat16)
        grad_in[h] = contract_first(tokens[0], units[1, h]).astype(jnp.bfloat16)
        stores.append(pltpu.make_async_copy(grad_out.at[h], w_out_grad.at[span], store_sem.at[h]))
        stores.append(pltpu.make_async_copy(grad_in.at[h], w_in_grad.at[:, span], store_sem.at[2 + h]))
        stores[-2].start()
        stores[-1].start()
    for k in range(2):
        wait(recv_out.at[k, pl.ds(0, COLS - 1)], out_recv.at[k])
        value = recv_out[k, 0].astype(jnp.float32)
        for source in range(1, COLS):
            value = value + recv_out[k, source].astype(jnp.float32)
        result[k] = value.astype(jnp.bfloat16)
        stores.append(pltpu.make_async_copy(result.at[k], (output, input_grad)[k], store_sem.at[4 + k]))
        stores[-1].start()

    for k in range(2):
        span = pl.ds(0, (COLS - 1) * BLOCK)
        wait(tokens.at[k, span], gather_send.at[k])
        wait(tokens_twin.at[k], pair_send.at[k])
        wait(sums.at[k, span], sum_send.at[k])
        wait(units.at[k, 0, span], unit_send.at[k])
        wait(units.at[k, 0], twin_send.at[k])
        wait(send_out.at[k, span], out_send.at[k])
    wait(w_in_twin, swap_send.at[0])
    wait(w_out_twin, swap_send.at[1])
    for copy in stores:
        copy.wait()


def place(*refs):
    pairs = list(zip(refs[:2], refs[4:6]))
    for source, target in zip(refs[2:4], refs[6:8]):
        count = source.shape[0] // PIECES
        spans = [pl.ds(i * count, count) for i in range(PIECES)]
        pairs += [(source.at[span], target.at[span]) for span in spans]
    copies = [pltpu.make_async_copy(source, target, refs[8].at[i]) for i, (source, target) in enumerate(pairs)]
    for copy in copies:
        copy.start()
    for copy in copies:
        copy.wait()


def exchange(inputs, w_in, w_out, cotangent):
    bf16, f32 = jnp.bfloat16, jnp.float32
    dma = pltpu.SemaphoreType.DMA
    hbm = pl.BlockSpec(memory_space=pltpu.HBM)
    shape = jax.ShapeDtypeStruct
    return pl.pallas_call(
        kernel,
        out_shape=(
            shape((BLOCK, DEPTH), bf16),
            shape((BLOCK, DEPTH), bf16),
            shape((DEPTH, UNITS), bf16),
            shape((UNITS, DEPTH), bf16),
        ),
        in_specs=[hbm] * 4,
        out_specs=(hbm,) * 4,
        scratch_shapes=[
            pltpu.VMEM((2, TOKENS, DEPTH), bf16),
            pltpu.VMEM((2, TOKENS, DEPTH), bf16),
            pltpu.VMEM((2, DEPTH, HALF), bf16),
            pltpu.VMEM((2, HALF, DEPTH), bf16),
            pltpu.VMEM((DEPTH, HALF), bf16),
            pltpu.VMEM((HALF, DEPTH), bf16),
            pltpu.VMEM((2, TOKENS, HALF), f32),
            pltpu.VMEM((2, TOKENS, HALF), bf16),
            pltpu.VMEM((2, TOKENS, HALF), bf16),
            pltpu.VMEM((2, 2, TOKENS, HALF), bf16),
            pltpu.VMEM((2, TOKENS, DEPTH), bf16),
            pltpu.VMEM((2, COLS, BLOCK, DEPTH), bf16),
            pltpu.VMEM((2, DEPTH, HALF), bf16),
            pltpu.VMEM((2, HALF, DEPTH), bf16),
            pltpu.VMEM((2, BLOCK, DEPTH), bf16),
            dma((6,)),
            dma((4,)), dma((2,)), dma((2,)), dma((2,)), dma((2,)), dma((2,)), dma((2,)), dma((2,)),
            dma((2,)), dma((2, 16)), dma((2,)), dma((2, 16)), dma((2,)), dma((2, 3)), dma((2,)), dma((2,)),
        ],
        compiler_params=pltpu.CompilerParams(
            collective_id=0, has_side_effects=True, vmem_limit_bytes=VMEM_LIMIT
        ),
        name="feed_forward",
    )(inputs, w_in, w_out, cotangent)


def local(inputs, w_in, w_out, cotangent):
    results = exchange(inputs, w_in, w_out, cotangent)
    return pl.pallas_call(
        place,
        out_shape=tuple(jax.ShapeDtypeStruct(result.shape, result.dtype) for result in results),
        in_specs=[pl.BlockSpec(memory_space=pltpu.HBM)] * 4,
        out_specs=(pl.BlockSpec(memory_space=pltpu.HBM),) * 4,
        scratch_shapes=[pltpu.SemaphoreType.DMA((2 + 2 * PIECES,))],
        compiler_params=pltpu.CompilerParams(vmem_limit_bytes=VMEM_LIMIT),
        name="place",
    )(*results)


def solution(mesh):
    placed = (P("col", "row"), P("row", "col"), P("col", "row"), P("col", "row"))
    return jax.shard_map(
        local,
        mesh=mesh,
        in_specs=placed,
        out_specs=(P("col", "row"), P("col", "row"), P("row", "col"), P("col", "row")),
        check_vma=False,
    )
```

```python
import jax
import jax.numpy as jnp
from jax import lax
from jax.experimental import pallas as pl
from jax.experimental.pallas import tpu as pltpu
from jax.sharding import PartitionSpec as P

MESH = pl.DeviceIdType.MESH
gelu_coef = 0.7978845608
cubic_coef = 0.044715

CHIPS = 16
COLS = 16
BLOCK = 16
TOKENS = 256
DEPTH = 384
UNITS = 1536
HALF = 768
PIECES = 4
VMEM_LIMIT = 58 * 1024 * 1024

SIDES = {
    3: 0, -3: 0, 1: 0, -1: 0, 6: 3, -6: -3, 4: 3, -4: -3, 2: 1, -2: -1, 7: 6, -7: -6, 5: 4, -5: -4,
}
PARENTS = (SIDES | {8: 6}, SIDES | {8: -6})


def children_of(parents):
    children = {}
    for child in sorted(parents, key=lambda role: -abs(role)):
        children.setdefault(parents[child], []).append(child)
    return children


def depth(role, parents):
    return 1 + depth(parents[role], parents) if role else 0


def height(role, children):
    return 1 + max((height(child, children) for child in children.get(role, ())), default=-1)


def levels(rank, parents, tree):
    found = {}
    for role in sorted(parents, key=lambda role: -abs(role)):
        found.setdefault(rank(role, tree), []).append(role)
    return [found[level] for level in sorted(found)]


CHILDREN = [children_of(parents) for parents in PARENTS]
SUM_LEVELS = [levels(height, parents, children) for parents, children in zip(PARENTS, CHILDREN)]
UNIT_LEVELS = [levels(depth, parents, parents) for parents in PARENTS]
FAR_FIRST = (
    (2, 2), (1, 2), (3, 2), (2, 1), (2, 3), (0, 2), (2, 0), (1, 1), (1, 3), (3, 1), (3, 3), (0, 1), (0, 3), (1, 0), (3, 0),
)
OFFSETS = sorted({(way * (tree[r] - r) + 8) % CHIPS - 8 for tree in PARENTS for r in tree for way in (1, -1)})
MIDDLE, LOW, HIGH = range(4, 12), range(0, 4), range(12, 16)


def rows(role):
    return pl.ds((role + 7) * BLOCK, BLOCK)


def contract_last(left, right):
    return lax.dot_general(
        left, right, (((1,), (1,)), ((), ())), preferred_element_type=jnp.float32
    )


def contract_first(left, right):
    return lax.dot_general(
        left, right, (((0,), (0,)), ((), ())), preferred_element_type=jnp.float32
    )


def kernel(
    inputs, w_in, w_out, cotangent,
    output, input_grad, w_in_grad, w_out_grad,
    tokens, tokens_twin, w_in_v, w_out_v, w_in_twin, w_out_twin, mine, sums, sums_in, units, send_out, recv_out,
    grad_in, grad_out, result, store_sem,
    load_sem, own_sem, gather_send, gather_recv, pair_send, pair_recv, swap_send, swap_recv, sum_send, sum_recv,
    unit_send, unit_recv, twin_send, twin_recv, out_send, out_recv,
):
    row, col = lax.axis_index("row"), lax.axis_index("col")
    z, c = row // 2, lax.rem(row, 2)
    twin = (z * 2 + 1 - c, col)

    def along(offset):
        return (lax.rem(z + offset + CHIPS, CHIPS) * 2 + c, col)

    def across(step):
        return (row, lax.rem(col // 4 + step[0], 4) * 4 + lax.rem(lax.rem(col, 4) + step[1], 4))

    def send(src, dst, send_sem, recv_sem, device):
        pltpu.make_async_remote_copy(
            src_ref=src, dst_ref=dst, send_sem=send_sem, recv_sem=recv_sem,
            device_id=device, device_id_type=MESH,
        ).start()

    def wait(ref, sem):
        pltpu.make_async_copy(ref, ref, sem).wait()

    here = pl.ds(pl.multiple_of(lax.rem(z - col + 7 + CHIPS, CHIPS) * BLOCK, BLOCK), BLOCK)

    own = [
        pltpu.make_async_copy(source, tokens.at[k, here], own_sem.at[k])
        for k, source in enumerate((inputs, cotangent))
    ]
    loads = [
        pltpu.make_async_copy(w_in.at[:, pl.ds(h * HALF, HALF)], w_in_v.at[h], load_sem.at[h])
        for h in range(2)
    ] + [pltpu.make_async_copy(w_out.at[pl.ds(h * HALF, HALF)], w_out_v.at[h], load_sem.at[2 + h]) for h in range(2)]
    for copy in own + loads:
        copy.start()

    barrier = pltpu.get_barrier_semaphore()
    peers = [across(step) for step in FAR_FIRST] + [along(offset) for offset in OFFSETS] + [twin]
    for peer in peers:
        pl.semaphore_signal(barrier, inc=1, device_id=peer, device_id_type=MESH)
    pl.semaphore_wait(barrier, len(peers))

    for k in range(2):
        own[k].wait()
        for step in FAR_FIRST:
            send(tokens.at[k, here], tokens.at[k, here], gather_send.at[k], gather_recv.at[k], across(step))
        if k == 0:
            theirs = w_in.at[:, pl.ds(pl.multiple_of((1 - c) * HALF, HALF), HALF)]
            send(theirs, w_in_twin, swap_send.at[0], swap_recv.at[0], twin)
        else:
            theirs = w_out.at[pl.ds(pl.multiple_of((1 - c) * HALF, HALF), HALF)]
            send(theirs, w_out_twin, swap_send.at[1], swap_recv.at[1], twin)
    for copy in loads:
        copy.wait()

    def first_round(k):
        wait(tokens.at[k, pl.ds(0, (COLS - 1) * BLOCK)], gather_recv.at[k])
        send(tokens.at[k], tokens_twin.at[k], pair_send.at[k], pair_recv.at[k], twin)
        if k == 0:
            mine[0] = jnp.dot(tokens[0], w_in_v[c], preferred_element_type=jnp.float32)
            wait(w_in_twin, swap_recv.at[0])
            wait(tokens_twin.at[0], pair_recv.at[0])
            mine[0] += jnp.dot(tokens_twin[0], w_in_twin[...], preferred_element_type=jnp.float32)
        else:
            mine[1] = contract_last(tokens[1], w_out_v[c])
            wait(w_out_twin, swap_recv.at[1])
            wait(tokens_twin.at[1], pair_recv.at[1])
            mine[1] += contract_last(tokens_twin[1], w_out_twin[...])
        for role in SUM_LEVELS[k][0]:
            pass_on(k, role)

    def collected(k, role):
        value = mine[k, rows(role)]
        for child in CHILDREN[k].get(role, ()):
            wait(sums_in.at[k, rows(child)], sum_recv.at[k, child + 7])
            value = value + sums_in[k, rows(child)].astype(jnp.float32)
        return value

    def pass_on(k, role):
        sums[k, rows(role)] = collected(k, role).astype(jnp.bfloat16)
        send(
            sums.at[k, rows(role)], sums_in.at[k, rows(role)], sum_send.at[k], sum_recv.at[k, role + 7],
            along(PARENTS[k][role] - role),
        )

    def hand_out(k, role):
        for child in CHILDREN[k].get(role, ()):
            send(
                units.at[k, c, rows(role)], units.at[k, c, rows(child)], unit_send.at[k], unit_recv.at[k, child + 7],
                along(child - role),
            )

    def hand_over(k, role):
        group = 0 if role + 7 in MIDDLE else 1 if role + 7 in LOW else 2
        send(units.at[k, c, rows(role)], units.at[k, c, rows(role)], twin_send.at[k], twin_recv.at[k, group], twin)

    def relay(k, roles):
        for role in roles:
            wait(units.at[k, c, rows(role)], unit_recv.at[k, role + 7])
            hand_out(k, role)
        for role in roles:
            hand_over(k, role)

    def unit_terms(k, group, blocks):
        span = pl.ds(blocks[0] * BLOCK, len(blocks) * BLOCK)
        wait(units.at[k, 1 - c, span], twin_recv.at[k, group])
        if k == 0:
            value = jnp.dot(units[0, 0, span], w_out_v[0], preferred_element_type=jnp.float32)
            value = value + jnp.dot(units[0, 1, span], w_out_v[1], preferred_element_type=jnp.float32)
        else:
            value = contract_last(units[1, 0, span], w_in_v[0])
            value = value + contract_last(units[1, 1, span], w_in_v[1])
        send_out[k, span] = value.astype(jnp.bfloat16)
        for p in blocks:
            target = lax.rem(z + 7 - p + CHIPS, CHIPS)
            source = send_out.at[k, pl.ds(p * BLOCK, BLOCK)]

            @pl.when(target != col)
            def _():
                send(source, recv_out.at[k, col], out_send.at[k], out_recv.at[k], (row, target))

            @pl.when(target == col)
            def _():
                recv_out[k, col] = source[...]

    first_round(0)
    first_round(1)
    for level in range(1, 3):
        for k in range(2):
            for role in SUM_LEVELS[k][level]:
                pass_on(k, role)

    pre_act = collected(0, 0)
    inner = jnp.tanh(gelu_coef * (pre_act + cubic_coef * pre_act * pre_act * pre_act))
    units[0, c, rows(0)] = (0.5 * pre_act * (1.0 + inner)).astype(jnp.bfloat16)
    hand_out(0, 0)
    hand_over(0, 0)
    slope = 0.5 * (1.0 + inner) + 0.5 * pre_act * (1.0 - inner * inner) * gelu_coef * (
        1.0 + 3.0 * cubic_coef * pre_act * pre_act
    )
    units[1, c, rows(0)] = (collected(1, 0) * slope).astype(jnp.bfloat16)
    hand_out(1, 0)
    hand_over(1, 0)

    for level in range(2):
        for k in range(2):
            relay(k, UNIT_LEVELS[k][level])
    for k in range(2):
        unit_terms(k, 0, MIDDLE)
        relay(k, UNIT_LEVELS[k][2])
    for k in range(2):
        unit_terms(k, 1, LOW)
        unit_terms(k, 2, HIGH)
    stores = []
    for h in range(2):
        span = pl.ds(h * HALF, HALF)
        grad_out[h] = contract_first(units[0, h], tokens[1]).astype(jnp.bfloat16)
        grad_in[h] = contract_first(tokens[0], units[1, h]).astype(jnp.bfloat16)
        stores.append(pltpu.make_async_copy(grad_out.at[h], w_out_grad.at[span], store_sem.at[h]))
        stores.append(pltpu.make_async_copy(grad_in.at[h], w_in_grad.at[:, span], store_sem.at[2 + h]))
        stores[-2].start()
        stores[-1].start()
    for k in range(2):
        wait(recv_out.at[k, pl.ds(0, COLS - 1)], out_recv.at[k])
        value = recv_out[k, 0].astype(jnp.float32)
        for source in range(1, COLS):
            value = value + recv_out[k, source].astype(jnp.float32)
        result[k] = value.astype(jnp.bfloat16)
        stores.append(pltpu.make_async_copy(result.at[k], (output, input_grad)[k], store_sem.at[4 + k]))
        stores[-1].start()

    for k in range(2):
        span = pl.ds(0, (COLS - 1) * BLOCK)
        wait(tokens.at[k, span], gather_send.at[k])
        wait(tokens_twin.at[k], pair_send.at[k])
        wait(sums.at[k, span], sum_send.at[k])
        wait(units.at[k, 0, span], unit_send.at[k])
        wait(units.at[k, 0], twin_send.at[k])
        wait(send_out.at[k, span], out_send.at[k])
    wait(w_in_twin, swap_send.at[0])
    wait(w_out_twin, swap_send.at[1])
    for copy in stores:
        copy.wait()


def place(*refs):
    pairs = list(zip(refs[:2], refs[8:10], refs[4:6]))
    for source, middle, target in zip(refs[2:4], refs[10:12], refs[6:8]):
        count = source.shape[0] // PIECES
        spans = [pl.ds(i * count, count) for i in range(PIECES)]
        pairs += [(source.at[span], middle.at[span], target.at[span]) for span in spans]
    reads = [pltpu.make_async_copy(pair[0], pair[1], refs[12].at[i]) for i, pair in enumerate(pairs)]
    writes = [pltpu.make_async_copy(pair[1], pair[2], refs[13].at[i]) for i, pair in enumerate(pairs)]
    for copy in reads:
        copy.start()
    for read, write in zip(reads, writes):
        read.wait()
        write.start()
    for copy in writes:
        copy.wait()


def exchange(inputs, w_in, w_out, cotangent):
    bf16, f32 = jnp.bfloat16, jnp.float32
    dma = pltpu.SemaphoreType.DMA
    hbm = pl.BlockSpec(memory_space=pltpu.HBM)
    shape = jax.ShapeDtypeStruct
    return pl.pallas_call(
        kernel,
        out_shape=(
            shape((BLOCK, DEPTH), bf16),
            shape((BLOCK, DEPTH), bf16),
            shape((DEPTH, UNITS), bf16),
            shape((UNITS, DEPTH), bf16),
        ),
        in_specs=[hbm] * 4,
        out_specs=(hbm,) * 4,
        scratch_shapes=[
            pltpu.VMEM((2, TOKENS, DEPTH), bf16),
            pltpu.VMEM((2, TOKENS, DEPTH), bf16),
            pltpu.VMEM((2, DEPTH, HALF), bf16),
            pltpu.VMEM((2, HALF, DEPTH), bf16),
            pltpu.VMEM((DEPTH, HALF), bf16),
            pltpu.VMEM((HALF, DEPTH), bf16),
            pltpu.VMEM((2, TOKENS, HALF), f32),
            pltpu.VMEM((2, TOKENS, HALF), bf16),
            pltpu.VMEM((2, TOKENS, HALF), bf16),
            pltpu.VMEM((2, 2, TOKENS, HALF), bf16),
            pltpu.VMEM((2, TOKENS, DEPTH), bf16),
            pltpu.VMEM((2, COLS, BLOCK, DEPTH), bf16),
            pltpu.VMEM((2, DEPTH, HALF), bf16),
            pltpu.VMEM((2, HALF, DEPTH), bf16),
            pltpu.VMEM((2, BLOCK, DEPTH), bf16),
            dma((6,)),
            dma((4,)), dma((2,)), dma((2,)), dma((2,)), dma((2,)), dma((2,)), dma((2,)), dma((2,)),
            dma((2,)), dma((2, 16)), dma((2,)), dma((2, 16)), dma((2,)), dma((2, 3)), dma((2,)), dma((2,)),
        ],
        compiler_params=pltpu.CompilerParams(
            collective_id=0, has_side_effects=True, vmem_limit_bytes=VMEM_LIMIT
        ),
        name="feed_forward",
    )(inputs, w_in, w_out, cotangent)


def local(inputs, w_in, w_out, cotangent):
    results = exchange(inputs, w_in, w_out, cotangent)
    return pl.pallas_call(
        place,
        out_shape=tuple(jax.ShapeDtypeStruct(result.shape, result.dtype) for result in results),
        in_specs=[pl.BlockSpec(memory_space=pltpu.HBM)] * 4,
        out_specs=(pl.BlockSpec(memory_space=pltpu.HBM),) * 4,
        scratch_shapes=[pltpu.VMEM(result.shape, result.dtype) for result in results]
        + [pltpu.SemaphoreType.DMA((2 + 2 * PIECES,))] * 2,
        compiler_params=pltpu.CompilerParams(vmem_limit_bytes=VMEM_LIMIT),
        name="place",
    )(*results)


def solution(mesh):
    placed = (P("col", "row"), P("row", "col"), P("col", "row"), P("col", "row"))
    return jax.shard_map(
        local,
        mesh=mesh,
        in_specs=placed,
        out_specs=(P("col", "row"), P("col", "row"), P("row", "col"), P("col", "row")),
        check_vma=False,
    )
```

```python
import jax
import jax.numpy as jnp
from jax import lax
from jax.experimental import pallas as pl
from jax.experimental.pallas import tpu as pltpu
from jax.sharding import PartitionSpec as P

MESH = pl.DeviceIdType.MESH
gelu_coef = 0.7978845608
cubic_coef = 0.044715

CHIPS = 16
COLS = 16
BLOCK = 16
TOKENS = 256
DEPTH = 384
UNITS = 1536
HALF = 768
PIECES = 4
VMEM_LIMIT = 32 * 1024 * 1024

SIDES = {
    3: 0, -3: 0, 1: 0, -1: 0, 6: 3, -6: -3, 4: 3, -4: -3, 2: 1, -2: -1, 7: 6, -7: -6, 5: 4, -5: -4,
}
PARENTS = (SIDES | {8: 6}, SIDES | {8: -6})


def children_of(parents):
    children = {}
    for child in sorted(parents, key=lambda role: -abs(role)):
        children.setdefault(parents[child], []).append(child)
    return children


def depth(role, parents):
    return 1 + depth(parents[role], parents) if role else 0


def height(role, children):
    return 1 + max((height(child, children) for child in children.get(role, ())), default=-1)


def levels(rank, parents, tree):
    found = {}
    for role in sorted(parents, key=lambda role: -abs(role)):
        found.setdefault(rank(role, tree), []).append(role)
    return [found[level] for level in sorted(found)]


CHILDREN = [children_of(parents) for parents in PARENTS]
SUM_LEVELS = [levels(height, parents, children) for parents, children in zip(PARENTS, CHILDREN)]
UNIT_LEVELS = [levels(depth, parents, parents) for parents in PARENTS]
FAR_FIRST = (
    (2, 2), (1, 2), (3, 2), (2, 1), (2, 3), (0, 2), (2, 0), (1, 1), (1, 3), (3, 1), (3, 3), (0, 1), (0, 3), (1, 0), (3, 0),
)
OFFSETS = sorted({(way * (tree[r] - r) + 8) % CHIPS - 8 for tree in PARENTS for r in tree for way in (1, -1)})
SHIFT = 3
NEAR, FAR = range(0, 8), range(8, 16)


def place_of(role):
    return (role + SHIFT) % CHIPS


def rows(role):
    return pl.ds(place_of(role) * BLOCK, BLOCK)


def contract_last(left, right):
    return lax.dot_general(
        left, right, (((1,), (1,)), ((), ())), preferred_element_type=jnp.float32
    )


def contract_first(left, right):
    return lax.dot_general(
        left, right, (((0,), (0,)), ((), ())), preferred_element_type=jnp.float32
    )


def kernel(
    inputs, w_in, w_out, cotangent,
    output, input_grad, w_in_grad, w_out_grad,
    tokens, tokens_twin, w_in_v, w_out_v, w_in_twin, w_out_twin, mine, sums, sums_in, units, send_out, recv_out,
    load_sem, own_sem, gather_send, gather_recv, pair_send, pair_recv, swap_send, swap_recv, sum_send, sum_recv,
    unit_send, unit_recv, twin_send, twin_recv, out_send, out_recv,
):
    row, col = lax.axis_index("row"), lax.axis_index("col")
    z, c = row // 2, lax.rem(row, 2)
    twin = (z * 2 + 1 - c, col)

    def along(offset):
        return (lax.rem(z + offset + CHIPS, CHIPS) * 2 + c, col)

    def across(step):
        return (row, lax.rem(col // 4 + step[0], 4) * 4 + lax.rem(lax.rem(col, 4) + step[1], 4))

    def send(src, dst, send_sem, recv_sem, device):
        pltpu.make_async_remote_copy(
            src_ref=src, dst_ref=dst, send_sem=send_sem, recv_sem=recv_sem,
            device_id=device, device_id_type=MESH,
        ).start()

    def wait(ref, sem):
        pltpu.make_async_copy(ref, ref, sem).wait()

    here_at = lax.rem(z - col + SHIFT + CHIPS, CHIPS)
    here = pl.ds(pl.multiple_of(here_at * BLOCK, BLOCK), BLOCK)

    own = [
        pltpu.make_async_copy(source, tokens.at[k, here], own_sem.at[k])
        for k, source in enumerate((inputs, cotangent))
    ]
    loads = [
        pltpu.make_async_copy(w_in.at[:, pl.ds(h * HALF, HALF)], w_in_v.at[h], load_sem.at[h])
        for h in range(2)
    ] + [pltpu.make_async_copy(w_out.at[pl.ds(h * HALF, HALF)], w_out_v.at[h], load_sem.at[2 + h]) for h in range(2)]
    for copy in own + loads:
        copy.start()

    barrier = pltpu.get_barrier_semaphore()
    peers = [across(step) for step in FAR_FIRST[:5]] + [along(offset) for offset in OFFSETS]
    peers += [across(step) for step in FAR_FIRST[5:]] + [twin]
    for peer in peers:
        pl.semaphore_signal(barrier, inc=1, device_id=peer, device_id_type=MESH)
    pl.semaphore_wait(barrier, len(peers))

    for k in range(2):
        own[k].wait()
        for step in FAR_FIRST:
            send(tokens.at[k, here], tokens.at[k, here], gather_send.at[k], gather_recv.at[k], across(step))
        if k == 0:
            theirs = w_in.at[:, pl.ds(pl.multiple_of((1 - c) * HALF, HALF), HALF)]
            send(theirs, w_in_twin, swap_send.at[0], swap_recv.at[0], twin)
        else:
            theirs = w_out.at[pl.ds(pl.multiple_of((1 - c) * HALF, HALF), HALF)]
            send(theirs, w_out_twin, swap_send.at[1], swap_recv.at[1], twin)
    for copy in loads:
        copy.wait()

    def swap_tokens(k):
        wait(tokens.at[k, pl.ds(0, (COLS - 1) * BLOCK)], gather_recv.at[k])
        send(tokens.at[k], tokens_twin.at[k], pair_send.at[k], pair_recv.at[k], twin)

    def width_terms(k):
        if k == 0:
            mine[0] = jnp.dot(tokens[0], w_in_v[c], preferred_element_type=jnp.float32)
            wait(w_in_twin, swap_recv.at[0])
            wait(tokens_twin.at[0], pair_recv.at[0])
            mine[0] += jnp.dot(tokens_twin[0], w_in_twin[...], preferred_element_type=jnp.float32)
        else:
            mine[1] = contract_last(tokens[1], w_out_v[c])
            wait(w_out_twin, swap_recv.at[1])
            wait(tokens_twin.at[1], pair_recv.at[1])
            mine[1] += contract_last(tokens_twin[1], w_out_twin[...])

    def collected(k, role):
        value = mine[k, rows(role)]
        for child in CHILDREN[k].get(role, ()):
            wait(sums_in.at[k, rows(child)], sum_recv.at[k, place_of(child)])
            value = value + sums_in[k, rows(child)].astype(jnp.float32)
        return value

    def pass_on(k, role):
        sums[k, rows(role)] = collected(k, role).astype(jnp.bfloat16)
        send(
            sums.at[k, rows(role)], sums_in.at[k, rows(role)], sum_send.at[k], sum_recv.at[k, place_of(role)],
            along(PARENTS[k][role] - role),
        )

    def hand_out(k, role):
        for child in CHILDREN[k].get(role, ()):
            send(
                units.at[k, c, rows(role)], units.at[k, c, rows(child)], unit_send.at[k], unit_recv.at[k, place_of(child)],
                along(child - role),
            )

    def hand_over(k, role):
        group = 0 if place_of(role) in NEAR else 1
        send(units.at[k, c, rows(role)], units.at[k, c, rows(role)], twin_send.at[k], twin_recv.at[k, group], twin)

    def relay(k, roles):
        for role in roles:
            wait(units.at[k, c, rows(role)], unit_recv.at[k, place_of(role)])
            hand_out(k, role)
        for role in roles:
            hand_over(k, role)

    def unit_terms(k, group):
        blocks = (NEAR, FAR)[group]
        span = pl.ds(blocks[0] * BLOCK, len(blocks) * BLOCK)

        def terms(h):
            if k == 0:
                return jnp.dot(units[0, h, span], w_out_v[h], preferred_element_type=jnp.float32)
            return contract_last(units[1, h, span], w_in_v[h])

        value = terms(c)
        wait(units.at[k, 1 - c, span], twin_recv.at[k, group])
        value = value + terms(1 - c)
        send_out[k, span] = value.astype(jnp.bfloat16)
        for step in FAR_FIRST:
            device = across(step)
            p = lax.rem(z - device[1] + SHIFT + CHIPS, CHIPS)

            @pl.when((p >= blocks[0]) & (p <= blocks[-1]))
            def _():
                block = pl.ds(pl.multiple_of(p * BLOCK, BLOCK), BLOCK)
                send(send_out.at[k, block], recv_out.at[k, col], out_send.at[k], out_recv.at[k], device)

        @pl.when((here_at >= blocks[0]) & (here_at <= blocks[-1]))
        def _():
            recv_out[k, col] = send_out[k, here]

    swap_tokens(0)
    width_terms(0)
    swap_tokens(1)
    for role in SUM_LEVELS[0][0]:
        pass_on(0, role)
    width_terms(1)
    for role in SUM_LEVELS[1][0]:
        pass_on(1, role)
    for level in range(1, 3):
        for k in range(2):
            for role in SUM_LEVELS[k][level]:
                pass_on(k, role)

    pre_act = collected(0, 0)
    inner = jnp.tanh(gelu_coef * (pre_act + cubic_coef * pre_act * pre_act * pre_act))
    units[0, c, rows(0)] = (0.5 * pre_act * (1.0 + inner)).astype(jnp.bfloat16)
    hand_out(0, 0)
    hand_over(0, 0)
    slope = 0.5 * (1.0 + inner) + 0.5 * pre_act * (1.0 - inner * inner) * gelu_coef * (
        1.0 + 3.0 * cubic_coef * pre_act * pre_act
    )
    units[1, c, rows(0)] = (collected(1, 0) * slope).astype(jnp.bfloat16)
    hand_out(1, 0)
    hand_over(1, 0)

    for level in range(2):
        for k in range(2):
            relay(k, UNIT_LEVELS[k][level])
    for k in range(2):
        unit_terms(k, 0)
        relay(k, UNIT_LEVELS[k][2])
    for k in range(2):
        unit_terms(k, 1)
    for h in range(2):
        span = pl.ds(h * HALF, HALF)
        w_out_grad[span] = contract_first(units[0, h], tokens[1]).astype(jnp.bfloat16)
        w_in_grad[:, span] = contract_first(tokens[0], units[1, h]).astype(jnp.bfloat16)
    for k in range(2):
        wait(recv_out.at[k, pl.ds(0, COLS - 1)], out_recv.at[k])
        value = recv_out[k, 0].astype(jnp.float32)
        for source in range(1, COLS):
            value = value + recv_out[k, source].astype(jnp.float32)
        (output, input_grad)[k][...] = value.astype(jnp.bfloat16)

    for k in range(2):
        span = pl.ds(0, (COLS - 1) * BLOCK)
        wait(tokens.at[k, span], gather_send.at[k])
        wait(tokens_twin.at[k], pair_send.at[k])
        wait(sums.at[k, span], sum_send.at[k])
        wait(units.at[k, 0, span], unit_send.at[k])
        wait(units.at[k, 0], twin_send.at[k])
        wait(send_out.at[k, span], out_send.at[k])
    wait(w_in_twin, swap_send.at[0])
    wait(w_out_twin, swap_send.at[1])


def place(*refs):
    pairs = list(zip(refs[:2], refs[4:6]))
    for source, target in zip(refs[2:4], refs[6:8]):
        count = source.shape[0] // PIECES
        spans = [pl.ds(i * count, count) for i in range(PIECES)]
        pairs += [(source.at[span], target.at[span]) for span in spans]
    copies = [pltpu.make_async_copy(source, target, refs[8].at[i]) for i, (source, target) in enumerate(pairs)]
    for copy in copies:
        copy.start()
    for copy in copies:
        copy.wait()


def exchange(inputs, w_in, w_out, cotangent):
    bf16, f32 = jnp.bfloat16, jnp.float32
    dma = pltpu.SemaphoreType.DMA
    hbm, vmem = pl.BlockSpec(memory_space=pltpu.HBM), pl.BlockSpec(memory_space=pltpu.VMEM)
    return pl.pallas_call(
        kernel,
        out_shape=(
            pltpu.VMEM((BLOCK, DEPTH), bf16),
            pltpu.VMEM((BLOCK, DEPTH), bf16),
            pltpu.VMEM((DEPTH, UNITS), bf16),
            pltpu.VMEM((UNITS, DEPTH), bf16),
        ),
        in_specs=[hbm] * 4,
        out_specs=(vmem,) * 4,
        scratch_shapes=[
            pltpu.VMEM((2, TOKENS, DEPTH), bf16),
            pltpu.VMEM((2, TOKENS, DEPTH), bf16),
            pltpu.VMEM((2, DEPTH, HALF), bf16),
            pltpu.VMEM((2, HALF, DEPTH), bf16),
            pltpu.VMEM((DEPTH, HALF), bf16),
            pltpu.VMEM((HALF, DEPTH), bf16),
            pltpu.VMEM((2, TOKENS, HALF), f32),
            pltpu.VMEM((2, TOKENS, HALF), bf16),
            pltpu.VMEM((2, TOKENS, HALF), bf16),
            pltpu.VMEM((2, 2, TOKENS, HALF), bf16),
            pltpu.VMEM((2, TOKENS, DEPTH), bf16),
            pltpu.VMEM((2, COLS, BLOCK, DEPTH), bf16),
            dma((4,)), dma((2,)), dma((2,)), dma((2,)), dma((2,)), dma((2,)), dma((2,)), dma((2,)),
            dma((2,)), dma((2, 16)), dma((2,)), dma((2, 16)), dma((2,)), dma((2, 2)), dma((2,)), dma((2,)),
        ],
        compiler_params=pltpu.CompilerParams(
            collective_id=0, has_side_effects=True, vmem_limit_bytes=VMEM_LIMIT
        ),
        name="feed_forward",
    )(inputs, w_in, w_out, cotangent)


def local(inputs, w_in, w_out, cotangent):
    held = [pltpu.with_memory_space_constraint(array, pltpu.HBM) for array in (inputs, w_in, w_out, cotangent)]
    results = [pltpu.with_memory_space_constraint(array, pltpu.VMEM) for array in exchange(*held)]
    return pl.pallas_call(
        place,
        out_shape=tuple(pltpu.HBM(result.shape, result.dtype) for result in results),
        in_specs=[pl.BlockSpec(memory_space=pltpu.VMEM)] * 4,
        out_specs=(pl.BlockSpec(memory_space=pltpu.HBM),) * 4,
        scratch_shapes=[pltpu.SemaphoreType.DMA((2 + 2 * PIECES,))],
        compiler_params=pltpu.CompilerParams(vmem_limit_bytes=1024 * 1024),
        name="place",
    )(*results)


def solution(mesh):
    placed = (P("col", "row"), P("row", "col"), P("col", "row"), P("col", "row"))
    return jax.shard_map(
        local,
        mesh=mesh,
        in_specs=placed,
        out_specs=(P("col", "row"), P("col", "row"), P("row", "col"), P("col", "row")),
        check_vma=False,
    )
```

```python
import jax
import jax.numpy as jnp
from jax import lax
from jax.experimental import pallas as pl
from jax.experimental.pallas import tpu as pltpu
from jax.sharding import PartitionSpec as P

MESH = pl.DeviceIdType.MESH
gelu_coef = 0.7978845608
cubic_coef = 0.044715

CHIPS = 16
COLS = 16
BLOCK = 16
TOKENS = 256
DEPTH = 384
UNITS = 1536
HALF = 768
PIECES = 4
PARTS = 2
WIDE = HALF // PARTS
VMEM_LIMIT = 32 * 1024 * 1024

SIDES = {
    3: 0, -3: 0, 1: 0, -1: 0, 6: 3, -6: -3, 4: 3, -4: -3, 2: 1, -2: -1, 7: 6, -7: -6, 5: 4, -5: -4,
}
PARENTS = (SIDES | {8: 6}, SIDES | {8: -6})


def children_of(parents):
    children = {}
    for child in sorted(parents, key=lambda role: -abs(role)):
        children.setdefault(parents[child], []).append(child)
    return children


def depth(role, parents):
    return 1 + depth(parents[role], parents) if role else 0


def height(role, children):
    return 1 + max((height(child, children) for child in children.get(role, ())), default=-1)


def levels(rank, parents, tree):
    found = {}
    for role in sorted(parents, key=lambda role: -abs(role)):
        found.setdefault(rank(role, tree), []).append(role)
    return [found[level] for level in sorted(found)]


CHILDREN = [children_of(parents) for parents in PARENTS]
SUM_LEVELS = [levels(height, parents, children) for parents, children in zip(PARENTS, CHILDREN)]
UNIT_LEVELS = [levels(depth, parents, parents) for parents in PARENTS]
FAR_FIRST = (
    (2, 2), (1, 2), (3, 2), (2, 1), (2, 3), (0, 2), (2, 0), (1, 1), (1, 3), (3, 1), (3, 3), (0, 1), (0, 3), (1, 0), (3, 0),
)
OFFSETS = sorted({(way * (tree[r] - r) + 8) % CHIPS - 8 for tree in PARENTS for r in tree for way in (1, -1)})
SHIFT = 3
NEAR, FAR = range(0, 8), range(8, 16)


def columns(q):
    return pl.ds(q * WIDE, WIDE)


def place_of(role):
    return (role + SHIFT) % CHIPS


def rows(role):
    return pl.ds(place_of(role) * BLOCK, BLOCK)


def contract_last(left, right):
    return lax.dot_general(
        left, right, (((1,), (1,)), ((), ())), preferred_element_type=jnp.float32
    )


def contract_first(left, right):
    return lax.dot_general(
        left, right, (((0,), (0,)), ((), ())), preferred_element_type=jnp.float32
    )


def kernel(
    inputs, w_in, w_out, cotangent,
    output, input_grad, w_in_grad, w_out_grad,
    tokens, tokens_twin, w_in_v, w_out_v, w_in_twin, w_out_twin, mine, sums, sums_in, units, send_out, recv_out,
    load_sem, own_sem, gather_send, gather_recv, pair_send, pair_recv, swap_send, swap_recv, sum_send, sum_recv,
    unit_send, unit_recv, twin_send, twin_recv, out_send, out_recv,
):
    row, col = lax.axis_index("row"), lax.axis_index("col")
    z, c = row // 2, lax.rem(row, 2)
    twin = (z * 2 + 1 - c, col)

    def along(offset):
        return (lax.rem(z + offset + CHIPS, CHIPS) * 2 + c, col)

    def across(step):
        return (row, lax.rem(col // 4 + step[0], 4) * 4 + lax.rem(lax.rem(col, 4) + step[1], 4))

    def send(src, dst, send_sem, recv_sem, device):
        pltpu.make_async_remote_copy(
            src_ref=src, dst_ref=dst, send_sem=send_sem, recv_sem=recv_sem,
            device_id=device, device_id_type=MESH,
        ).start()

    def wait(ref, sem):
        pltpu.make_async_copy(ref, ref, sem).wait()

    here_at = lax.rem(z - col + SHIFT + CHIPS, CHIPS)
    here = pl.ds(pl.multiple_of(here_at * BLOCK, BLOCK), BLOCK)

    own = [
        pltpu.make_async_copy(source, tokens.at[k, here], own_sem.at[k])
        for k, source in enumerate((inputs, cotangent))
    ]
    loads = [
        pltpu.make_async_copy(w_in.at[:, pl.ds(h * HALF, HALF)], w_in_v.at[h], load_sem.at[h])
        for h in range(2)
    ] + [pltpu.make_async_copy(w_out.at[pl.ds(h * HALF, HALF)], w_out_v.at[h], load_sem.at[2 + h]) for h in range(2)]
    for copy in own + loads:
        copy.start()

    barrier = pltpu.get_barrier_semaphore()
    peers = [across(step) for step in FAR_FIRST[:5]] + [along(offset) for offset in OFFSETS]
    peers += [across(step) for step in FAR_FIRST[5:]] + [twin]
    for peer in peers:
        pl.semaphore_signal(barrier, inc=1, device_id=peer, device_id_type=MESH)
    pl.semaphore_wait(barrier, len(peers))

    for k in range(2):
        own[k].wait()
        for step in FAR_FIRST:
            send(tokens.at[k, here], tokens.at[k, here], gather_send.at[k], gather_recv.at[k], across(step))
        if k == 0:
            theirs = w_in.at[:, pl.ds(pl.multiple_of((1 - c) * HALF, HALF), HALF)]
            send(theirs, w_in_twin, swap_send.at[0], swap_recv.at[0], twin)
        else:
            theirs = w_out.at[pl.ds(pl.multiple_of((1 - c) * HALF, HALF), HALF)]
            send(theirs, w_out_twin, swap_send.at[1], swap_recv.at[1], twin)
    for copy in loads:
        copy.wait()

    def swap_tokens(k):
        wait(tokens.at[k, pl.ds(0, (COLS - 1) * BLOCK)], gather_recv.at[k])
        send(tokens.at[k], tokens_twin.at[k], pair_send.at[k], pair_recv.at[k], twin)

    def width_terms(k):
        for q in range(PARTS):
            if k == 0:
                mine[0, :, columns(q)] = jnp.dot(
                    tokens[0], w_in_v[c, :, columns(q)], preferred_element_type=jnp.float32
                )
            else:
                mine[1, :, columns(q)] = contract_last(tokens[1], w_out_v[c, columns(q)])
        wait((w_in_twin, w_out_twin)[k], swap_recv.at[k])
        wait(tokens_twin.at[k], pair_recv.at[k])
        for q in range(PARTS):
            if k == 0:
                mine[0, :, columns(q)] += jnp.dot(
                    tokens_twin[0], w_in_twin[:, columns(q)], preferred_element_type=jnp.float32
                )
            else:
                mine[1, :, columns(q)] += contract_last(tokens_twin[1], w_out_twin[columns(q)])
            for role in SUM_LEVELS[k][0]:
                pass_on(k, q, role)

    def collected(k, q, role):
        value = mine[k, rows(role), columns(q)]
        for child in CHILDREN[k].get(role, ()):
            wait(sums_in.at[k, rows(child), columns(q)], sum_recv.at[k, q, place_of(child)])
            value = value + sums_in[k, rows(child), columns(q)].astype(jnp.float32)
        return value

    def pass_on(k, q, role):
        sums[k, rows(role), columns(q)] = collected(k, q, role).astype(jnp.bfloat16)
        send(
            sums.at[k, rows(role), columns(q)], sums_in.at[k, rows(role), columns(q)], sum_send.at[k],
            sum_recv.at[k, q, place_of(role)], along(PARENTS[k][role] - role),
        )

    def hand_out(k, q, role):
        for child in CHILDREN[k].get(role, ()):
            send(
                units.at[k, c, rows(role), columns(q)], units.at[k, c, rows(child), columns(q)], unit_send.at[k],
                unit_recv.at[k, q, place_of(child)], along(child - role),
            )

    def hand_over(k, q, role):
        group = 0 if place_of(role) in NEAR else 1
        part = units.at[k, c, rows(role), columns(q)]
        send(part, part, twin_send.at[k], twin_recv.at[k, group], twin)

    def relay(k, roles):
        for q in range(PARTS):
            for role in roles:
                wait(units.at[k, c, rows(role), columns(q)], unit_recv.at[k, q, place_of(role)])
                hand_out(k, q, role)
            for role in roles:
                hand_over(k, q, role)

    def unit_terms(k, group):
        blocks = (NEAR, FAR)[group]
        span = pl.ds(blocks[0] * BLOCK, len(blocks) * BLOCK)

        def terms(h):
            if k == 0:
                return jnp.dot(units[0, h, span], w_out_v[h], preferred_element_type=jnp.float32)
            return contract_last(units[1, h, span], w_in_v[h])

        value = terms(c)
        wait(units.at[k, 1 - c, span], twin_recv.at[k, group])
        value = value + terms(1 - c)
        send_out[k, span] = value.astype(jnp.bfloat16)
        for step in FAR_FIRST:
            device = across(step)
            p = lax.rem(z - device[1] + SHIFT + CHIPS, CHIPS)

            @pl.when((p >= blocks[0]) & (p <= blocks[-1]))
            def _():
                block = pl.ds(pl.multiple_of(p * BLOCK, BLOCK), BLOCK)
                send(send_out.at[k, block], recv_out.at[k, col], out_send.at[k], out_recv.at[k], device)

        @pl.when((here_at >= blocks[0]) & (here_at <= blocks[-1]))
        def _():
            recv_out[k, col] = send_out[k, here]

    swap_tokens(0)
    width_terms(0)
    swap_tokens(1)
    width_terms(1)
    for level in range(1, 3):
        for k in range(2):
            for q in range(PARTS):
                for role in SUM_LEVELS[k][level]:
                    pass_on(k, q, role)

    slopes = []
    for q in range(PARTS):
        pre_act = collected(0, q, 0)
        inner = jnp.tanh(gelu_coef * (pre_act + cubic_coef * pre_act * pre_act * pre_act))
        units[0, c, rows(0), columns(q)] = (0.5 * pre_act * (1.0 + inner)).astype(jnp.bfloat16)
        hand_out(0, q, 0)
        hand_over(0, q, 0)
        slopes.append(
            0.5 * (1.0 + inner)
            + 0.5 * pre_act * (1.0 - inner * inner) * gelu_coef * (1.0 + 3.0 * cubic_coef * pre_act * pre_act)
        )
    for q in range(PARTS):
        units[1, c, rows(0), columns(q)] = (collected(1, q, 0) * slopes[q]).astype(jnp.bfloat16)
        hand_out(1, q, 0)
        hand_over(1, q, 0)

    for level in range(2):
        for k in range(2):
            relay(k, UNIT_LEVELS[k][level])
    unit_terms(0, 0)
    relay(0, UNIT_LEVELS[0][2])
    unit_terms(1, 0)
    unit_terms(0, 1)
    relay(1, UNIT_LEVELS[1][2])
    unit_terms(1, 1)
    for h in range(2):
        span = pl.ds(h * HALF, HALF)
        w_out_grad[span] = contract_first(units[0, h], tokens[1]).astype(jnp.bfloat16)
        w_in_grad[:, span] = contract_first(tokens[0], units[1, h]).astype(jnp.bfloat16)
    for k in range(2):
        wait(recv_out.at[k, pl.ds(0, COLS - 1)], out_recv.at[k])
        value = recv_out[k, 0].astype(jnp.float32)
        for source in range(1, COLS):
            value = value + recv_out[k, source].astype(jnp.float32)
        (output, input_grad)[k][...] = value.astype(jnp.bfloat16)

    for k in range(2):
        span = pl.ds(0, (COLS - 1) * BLOCK)
        wait(tokens.at[k, span], gather_send.at[k])
        wait(tokens_twin.at[k], pair_send.at[k])
        wait(sums.at[k, span], sum_send.at[k])
        wait(units.at[k, 0, span], unit_send.at[k])
        wait(units.at[k, 0], twin_send.at[k])
        wait(send_out.at[k, span], out_send.at[k])
    wait(w_in_twin, swap_send.at[0])
    wait(w_out_twin, swap_send.at[1])


def place(*refs):
    pairs = list(zip(refs[:2], refs[4:6]))
    for source, target in zip(refs[2:4], refs[6:8]):
        count = source.shape[0] // PIECES
        spans = [pl.ds(i * count, count) for i in range(PIECES)]
        pairs += [(source.at[span], target.at[span]) for span in spans]
    copies = [pltpu.make_async_copy(source, target, refs[8].at[i]) for i, (source, target) in enumerate(pairs)]
    for copy in copies:
        copy.start()
    for copy in copies:
        copy.wait()


def exchange(inputs, w_in, w_out, cotangent):
    bf16, f32 = jnp.bfloat16, jnp.float32
    dma = pltpu.SemaphoreType.DMA
    hbm, vmem = pl.BlockSpec(memory_space=pltpu.HBM), pl.BlockSpec(memory_space=pltpu.VMEM)
    return pl.pallas_call(
        kernel,
        out_shape=(
            pltpu.VMEM((BLOCK, DEPTH), bf16),
            pltpu.VMEM((BLOCK, DEPTH), bf16),
            pltpu.VMEM((DEPTH, UNITS), bf16),
            pltpu.VMEM((UNITS, DEPTH), bf16),
        ),
        in_specs=[hbm] * 4,
        out_specs=(vmem,) * 4,
        scratch_shapes=[
            pltpu.VMEM((2, TOKENS, DEPTH), bf16),
            pltpu.VMEM((2, TOKENS, DEPTH), bf16),
            pltpu.VMEM((2, DEPTH, HALF), bf16),
            pltpu.VMEM((2, HALF, DEPTH), bf16),
            pltpu.VMEM((DEPTH, HALF), bf16),
            pltpu.VMEM((HALF, DEPTH), bf16),
            pltpu.VMEM((2, TOKENS, HALF), f32),
            pltpu.VMEM((2, TOKENS, HALF), bf16),
            pltpu.VMEM((2, TOKENS, HALF), bf16),
            pltpu.VMEM((2, 2, TOKENS, HALF), bf16),
            pltpu.VMEM((2, TOKENS, DEPTH), bf16),
            pltpu.VMEM((2, COLS, BLOCK, DEPTH), bf16),
            dma((4,)), dma((2,)), dma((2,)), dma((2,)), dma((2,)), dma((2,)), dma((2,)), dma((2,)),
            dma((2,)), dma((2, PARTS, 16)), dma((2,)), dma((2, PARTS, 16)), dma((2,)), dma((2, 2)), dma((2,)), dma((2,)),
        ],
        compiler_params=pltpu.CompilerParams(
            collective_id=0, has_side_effects=True, vmem_limit_bytes=VMEM_LIMIT
        ),
        name="feed_forward",
    )(inputs, w_in, w_out, cotangent)


def local(inputs, w_in, w_out, cotangent):
    held = [pltpu.with_memory_space_constraint(array, pltpu.HBM) for array in (inputs, w_in, w_out, cotangent)]
    results = [pltpu.with_memory_space_constraint(array, pltpu.VMEM) for array in exchange(*held)]
    return pl.pallas_call(
        place,
        out_shape=tuple(pltpu.HBM(result.shape, result.dtype) for result in results),
        in_specs=[pl.BlockSpec(memory_space=pltpu.VMEM)] * 4,
        out_specs=(pl.BlockSpec(memory_space=pltpu.HBM),) * 4,
        scratch_shapes=[pltpu.SemaphoreType.DMA((2 + 2 * PIECES,))],
        compiler_params=pltpu.CompilerParams(vmem_limit_bytes=1024 * 1024),
        name="place",
    )(*results)


def solution(mesh):
    placed = (P("col", "row"), P("row", "col"), P("col", "row"), P("col", "row"))
    return jax.shard_map(
        local,
        mesh=mesh,
        in_specs=placed,
        out_specs=(P("col", "row"), P("col", "row"), P("row", "col"), P("col", "row")),
        check_vma=False,
    )
```

```python
import jax
import jax.numpy as jnp
from jax import lax
from jax.experimental import pallas as pl
from jax.experimental.pallas import tpu as pltpu
from jax.sharding import PartitionSpec as P

MESH = pl.DeviceIdType.MESH
gelu_coef = 0.7978845608
cubic_coef = 0.044715

CHIPS = 16
COLS = 16
BLOCK = 16
TOKENS = 256
DEPTH = 384
UNITS = 1536
HALF = 768
PIECES = 4
PARTS = 2
WIDE = HALF // PARTS
VMEM_LIMIT = 32 * 1024 * 1024

SIDES = {
    3: 0, -3: 0, 1: 0, -1: 0, 6: 3, -6: -3, 4: 3, -4: -3, 2: 1, -2: -1, 7: 6, -7: -6, 5: 4, -5: -4,
}
PARENTS = (SIDES | {8: 6}, SIDES | {8: -6})


def children_of(parents):
    children = {}
    for child in sorted(parents, key=lambda role: -abs(role)):
        children.setdefault(parents[child], []).append(child)
    return children


def depth(role, parents):
    return 1 + depth(parents[role], parents) if role else 0


def levels(parents):
    found = {}
    for role in sorted(parents, key=lambda role: -abs(role)):
        found.setdefault(depth(role, parents), []).append(role)
    return [found[level] for level in sorted(found)]


CHILDREN = [children_of(parents) for parents in PARENTS]
UNIT_LEVELS = [levels(parents) for parents in PARENTS]
SUM_LEVELS = [found[::-1] for found in UNIT_LEVELS]
FAR_FIRST = (
    (2, 2), (1, 2), (3, 2), (2, 1), (2, 3), (0, 2), (2, 0), (1, 1), (1, 3), (3, 1), (3, 3), (0, 1), (0, 3), (1, 0), (3, 0),
)
OFFSETS = sorted({(way * (tree[r] - r) + 8) % CHIPS - 8 for tree in PARENTS for r in tree for way in (1, -1)})
SHIFT = 3
NEAR, FAR = range(0, 8), range(8, 16)


def columns(q):
    return pl.ds(q * WIDE, WIDE)


def place_of(role):
    return (role + SHIFT) % CHIPS


def rows(role):
    return pl.ds(place_of(role) * BLOCK, BLOCK)


def contract_last(left, right):
    return lax.dot_general(
        left, right, (((1,), (1,)), ((), ())), preferred_element_type=jnp.float32
    )


def contract_first(left, right):
    return lax.dot_general(
        left, right, (((0,), (0,)), ((), ())), preferred_element_type=jnp.float32
    )


def kernel(
    inputs, w_in, w_out, cotangent,
    output, input_grad, w_in_grad, w_out_grad,
    tokens, tokens_twin, w_in_v, w_out_v, w_in_twin, w_out_twin, mine, sums, sums_in, units, send_out, recv_out,
    load_sem, own_sem, gather_send, gather_recv, pair_send, pair_recv, swap_send, swap_recv, sum_send, sum_recv,
    unit_send, unit_recv, twin_send, twin_recv, out_send, out_recv,
):
    row, col = lax.axis_index("row"), lax.axis_index("col")
    z, c = row // 2, lax.rem(row, 2)
    twin = (z * 2 + 1 - c, col)

    def along(offset):
        return (lax.rem(z + offset + CHIPS, CHIPS) * 2 + c, col)

    def across(step):
        return (row, lax.rem(col // 4 + step[0], 4) * 4 + lax.rem(lax.rem(col, 4) + step[1], 4))

    def send(src, dst, send_sem, recv_sem, device):
        pltpu.make_async_remote_copy(
            src_ref=src, dst_ref=dst, send_sem=send_sem, recv_sem=recv_sem,
            device_id=device, device_id_type=MESH,
        ).start()

    def wait(ref, sem):
        pltpu.make_async_copy(ref, ref, sem).wait()

    here_at = lax.rem(z - col + SHIFT + CHIPS, CHIPS)
    here = pl.ds(pl.multiple_of(here_at * BLOCK, BLOCK), BLOCK)

    own = [
        pltpu.make_async_copy(source, tokens.at[k, here], own_sem.at[k])
        for k, source in enumerate((inputs, cotangent))
    ]
    loads = [
        pltpu.make_async_copy(w_in.at[:, pl.ds(h * HALF, HALF)], w_in_v.at[h], load_sem.at[h])
        for h in range(2)
    ] + [pltpu.make_async_copy(w_out.at[pl.ds(h * HALF, HALF)], w_out_v.at[h], load_sem.at[2 + h]) for h in range(2)]
    for copy in own + loads:
        copy.start()

    barrier = pltpu.get_barrier_semaphore()
    peers = [across(step) for step in FAR_FIRST[:5]] + [along(offset) for offset in OFFSETS]
    peers += [across(step) for step in FAR_FIRST[5:]] + [twin]
    for peer in peers:
        pl.semaphore_signal(barrier, inc=1, device_id=peer, device_id_type=MESH)
    pl.semaphore_wait(barrier, len(peers))

    for k in range(2):
        own[k].wait()
        for step in FAR_FIRST:
            send(tokens.at[k, here], tokens.at[k, here], gather_send.at[k], gather_recv.at[k], across(step))
        if k == 0:
            theirs = w_in.at[:, pl.ds(pl.multiple_of((1 - c) * HALF, HALF), HALF)]
            send(theirs, w_in_twin, swap_send.at[0], swap_recv.at[0], twin)
        else:
            theirs = w_out.at[pl.ds(pl.multiple_of((1 - c) * HALF, HALF), HALF)]
            send(theirs, w_out_twin, swap_send.at[1], swap_recv.at[1], twin)
    for copy in loads:
        copy.wait()

    def swap_tokens(k):
        wait(tokens.at[k, pl.ds(0, (COLS - 1) * BLOCK)], gather_recv.at[k])
        send(tokens.at[k], tokens_twin.at[k], pair_send.at[k], pair_recv.at[k], twin)

    def width_terms(k):
        for q in range(PARTS):
            if k == 0:
                mine[0, :, columns(q)] = jnp.dot(
                    tokens[0], w_in_v[c, :, columns(q)], preferred_element_type=jnp.float32
                )
            else:
                mine[1, :, columns(q)] = contract_last(tokens[1], w_out_v[c, columns(q)])
        wait((w_in_twin, w_out_twin)[k], swap_recv.at[k])
        wait(tokens_twin.at[k], pair_recv.at[k])
        for q in range(PARTS):
            if k == 0:
                mine[0, :, columns(q)] += jnp.dot(
                    tokens_twin[0], w_in_twin[:, columns(q)], preferred_element_type=jnp.float32
                )
            else:
                mine[1, :, columns(q)] += contract_last(tokens_twin[1], w_out_twin[columns(q)])
            for role in SUM_LEVELS[k][0]:
                pass_on(k, q, role)

    def collected(k, q, role):
        value = mine[k, rows(role), columns(q)]
        for child in CHILDREN[k].get(role, ()):
            wait(sums_in.at[k, rows(child), columns(q)], sum_recv.at[k, q, place_of(child)])
            value = value + sums_in[k, rows(child), columns(q)].astype(jnp.float32)
        return value

    def pass_on(k, q, role):
        sums[k, rows(role), columns(q)] = collected(k, q, role).astype(jnp.bfloat16)
        send(
            sums.at[k, rows(role), columns(q)], sums_in.at[k, rows(role), columns(q)], sum_send.at[k],
            sum_recv.at[k, q, place_of(role)], along(PARENTS[k][role] - role),
        )

    def hand_out(k, q, role):
        for child in CHILDREN[k].get(role, ()):
            send(
                units.at[k, c, rows(role), columns(q)], units.at[k, c, rows(child), columns(q)], unit_send.at[k],
                unit_recv.at[k, q, place_of(child)], along(child - role),
            )

    def hand_over(k, q, role):
        group = 0 if place_of(role) in NEAR else 1
        part = units.at[k, c, rows(role), columns(q)]
        send(part, part, twin_send.at[k], twin_recv.at[k, group], twin)

    def relay(k, roles):
        for q in range(PARTS):
            for role in roles:
                wait(units.at[k, c, rows(role), columns(q)], unit_recv.at[k, q, place_of(role)])
                hand_out(k, q, role)
            for role in roles:
                hand_over(k, q, role)

    def unit_terms(k, group):
        blocks = (NEAR, FAR)[group]
        span = pl.ds(blocks[0] * BLOCK, len(blocks) * BLOCK)

        def terms(h):
            if k == 0:
                return jnp.dot(units[0, h, span], w_out_v[h], preferred_element_type=jnp.float32)
            return contract_last(units[1, h, span], w_in_v[h])

        value = terms(c)
        wait(units.at[k, 1 - c, span], twin_recv.at[k, group])
        value = value + terms(1 - c)
        send_out[k, span] = value.astype(jnp.bfloat16)
        for step in FAR_FIRST:
            device = across(step)
            p = lax.rem(z - device[1] + SHIFT + CHIPS, CHIPS)

            @pl.when((p >= blocks[0]) & (p <= blocks[-1]))
            def _():
                block = pl.ds(pl.multiple_of(p * BLOCK, BLOCK), BLOCK)
                send(send_out.at[k, block], recv_out.at[k, col], out_send.at[k], out_recv.at[k], device)

        @pl.when((here_at >= blocks[0]) & (here_at <= blocks[-1]))
        def _():
            recv_out[k, col] = send_out[k, here]

    swap_tokens(0)
    width_terms(0)
    swap_tokens(1)
    width_terms(1)
    for level in range(1, 3):
        for k in range(2):
            for q in range(PARTS):
                for role in SUM_LEVELS[k][level]:
                    pass_on(k, q, role)

    slopes = []
    for q in range(PARTS):
        pre_act = collected(0, q, 0)
        inner = jnp.tanh(gelu_coef * (pre_act + cubic_coef * pre_act * pre_act * pre_act))
        units[0, c, rows(0), columns(q)] = (0.5 * pre_act * (1.0 + inner)).astype(jnp.bfloat16)
        hand_out(0, q, 0)
        hand_over(0, q, 0)
        slopes.append(
            0.5 * (1.0 + inner)
            + 0.5 * pre_act * (1.0 - inner * inner) * gelu_coef * (1.0 + 3.0 * cubic_coef * pre_act * pre_act)
        )
    for q in range(PARTS):
        units[1, c, rows(0), columns(q)] = (collected(1, q, 0) * slopes[q]).astype(jnp.bfloat16)
        hand_out(1, q, 0)
        hand_over(1, q, 0)

    for level in range(2):
        for k in range(2):
            relay(k, UNIT_LEVELS[k][level])
    unit_terms(0, 0)
    relay(0, UNIT_LEVELS[0][2])
    unit_terms(1, 0)
    unit_terms(0, 1)
    relay(1, UNIT_LEVELS[1][2])
    unit_terms(1, 1)
    for h in range(2):
        span = pl.ds(h * HALF, HALF)
        w_out_grad[span] = contract_first(units[0, h], tokens[1]).astype(jnp.bfloat16)
        w_in_grad[:, span] = contract_first(tokens[0], units[1, h]).astype(jnp.bfloat16)
    for k in range(2):
        wait(recv_out.at[k, pl.ds(0, COLS - 1)], out_recv.at[k])
        value = recv_out[k, 0].astype(jnp.float32)
        for source in range(1, COLS):
            value = value + recv_out[k, source].astype(jnp.float32)
        (output, input_grad)[k][...] = value.astype(jnp.bfloat16)

    for k in range(2):
        span = pl.ds(0, (COLS - 1) * BLOCK)
        wait(tokens.at[k, span], gather_send.at[k])
        wait(tokens_twin.at[k], pair_send.at[k])
        wait(sums.at[k, span], sum_send.at[k])
        wait(units.at[k, 0, span], unit_send.at[k])
        wait(units.at[k, 0], twin_send.at[k])
        wait(send_out.at[k, span], out_send.at[k])
    wait(w_in_twin, swap_send.at[0])
    wait(w_out_twin, swap_send.at[1])


def place(*refs):
    pairs = list(zip(refs[:2], refs[4:6]))
    for source, target in zip(refs[2:4], refs[6:8]):
        count = source.shape[0] // PIECES
        spans = [pl.ds(i * count, count) for i in range(PIECES)]
        pairs += [(source.at[span], target.at[span]) for span in spans]
    copies = [pltpu.make_async_copy(source, target, refs[8].at[i]) for i, (source, target) in enumerate(pairs)]
    for copy in copies:
        copy.start()
    for copy in copies:
        copy.wait()


def exchange(inputs, w_in, w_out, cotangent):
    bf16, f32 = jnp.bfloat16, jnp.float32
    dma = pltpu.SemaphoreType.DMA
    hbm, vmem = pl.BlockSpec(memory_space=pltpu.HBM), pl.BlockSpec(memory_space=pltpu.VMEM)
    return pl.pallas_call(
        kernel,
        out_shape=(
            pltpu.VMEM((BLOCK, DEPTH), bf16),
            pltpu.VMEM((BLOCK, DEPTH), bf16),
            pltpu.VMEM((DEPTH, UNITS), bf16),
            pltpu.VMEM((UNITS, DEPTH), bf16),
        ),
        in_specs=[hbm] * 4,
        out_specs=(vmem,) * 4,
        scratch_shapes=[
            pltpu.VMEM((2, TOKENS, DEPTH), bf16),
            pltpu.VMEM((2, TOKENS, DEPTH), bf16),
            pltpu.VMEM((2, DEPTH, HALF), bf16),
            pltpu.VMEM((2, HALF, DEPTH), bf16),
            pltpu.VMEM((DEPTH, HALF), bf16),
            pltpu.VMEM((HALF, DEPTH), bf16),
            pltpu.VMEM((2, TOKENS, HALF), f32),
            pltpu.VMEM((2, TOKENS, HALF), bf16),
            pltpu.VMEM((2, TOKENS, HALF), bf16),
            pltpu.VMEM((2, 2, TOKENS, HALF), bf16),
            pltpu.VMEM((2, TOKENS, DEPTH), bf16),
            pltpu.VMEM((2, COLS, BLOCK, DEPTH), bf16),
            dma((4,)), dma((2,)), dma((2,)), dma((2,)), dma((2,)), dma((2,)), dma((2,)), dma((2,)),
            dma((2,)), dma((2, PARTS, 16)), dma((2,)), dma((2, PARTS, 16)), dma((2,)), dma((2, 2)), dma((2,)), dma((2,)),
        ],
        compiler_params=pltpu.CompilerParams(
            collective_id=0, has_side_effects=True, vmem_limit_bytes=VMEM_LIMIT
        ),
        name="feed_forward",
    )(inputs, w_in, w_out, cotangent)


def local(inputs, w_in, w_out, cotangent):
    held = [pltpu.with_memory_space_constraint(array, pltpu.HBM) for array in (inputs, w_in, w_out, cotangent)]
    results = [pltpu.with_memory_space_constraint(array, pltpu.VMEM) for array in exchange(*held)]
    return pl.pallas_call(
        place,
        out_shape=tuple(pltpu.HBM(result.shape, result.dtype) for result in results),
        in_specs=[pl.BlockSpec(memory_space=pltpu.VMEM)] * 4,
        out_specs=(pl.BlockSpec(memory_space=pltpu.HBM),) * 4,
        scratch_shapes=[pltpu.SemaphoreType.DMA((2 + 2 * PIECES,))],
        compiler_params=pltpu.CompilerParams(vmem_limit_bytes=1024 * 1024),
        name="place",
    )(*results)


def solution(mesh):
    placed = (P("col", "row"), P("row", "col"), P("col", "row"), P("col", "row"))
    return jax.shard_map(
        local,
        mesh=mesh,
        in_specs=placed,
        out_specs=(P("col", "row"), P("col", "row"), P("row", "col"), P("col", "row")),
        check_vma=False,
    )
```

```python
import jax
import jax.numpy as jnp
from jax import lax
from jax.experimental import pallas as pl
from jax.experimental.pallas import tpu as pltpu
from jax.sharding import PartitionSpec as P

MESH = pl.DeviceIdType.MESH
gelu_coef = 0.7978845608
cubic_coef = 0.044715

CHIPS = 16
COLS = 16
BLOCK = 16
TOKENS = 256
DEPTH = 384
UNITS = 1536
HALF = 768
PIECES = 4
PARTS = 2
WIDE = HALF // PARTS
VMEM_LIMIT = 32 * 1024 * 1024

SIDES = {
    3: 0, -3: 0, 1: 0, -1: 0, 6: 3, -6: -3, 4: 3, -4: -3, 2: 1, -2: -1, 7: 6, -7: -6, 5: 4, -5: -4,
}
PARENTS = (SIDES | {8: 6}, SIDES | {8: -6})


def children_of(parents):
    children = {}
    for child in sorted(parents, key=lambda role: -abs(role)):
        children.setdefault(parents[child], []).append(child)
    return children


def depth(role, parents):
    return 1 + depth(parents[role], parents) if role else 0


def levels(parents):
    found = {}
    for role in sorted(parents, key=lambda role: -abs(role)):
        found.setdefault(depth(role, parents), []).append(role)
    return [found[level] for level in sorted(found)]


CHILDREN = [children_of(parents) for parents in PARENTS]
UNIT_LEVELS = levels(PARENTS[0])
SUM_LEVELS = UNIT_LEVELS[::-1]
FAR_FIRST = (
    (2, 2), (1, 2), (3, 2), (2, 1), (2, 3), (0, 2), (2, 0), (1, 1), (1, 3), (3, 1), (3, 3), (0, 1), (0, 3), (1, 0), (3, 0),
)
OFFSETS = sorted({(way * (tree[r] - r) + 8) % CHIPS - 8 for tree in PARENTS for r in tree for way in (1, -1)})
SHIFT = 3
NEAR, FAR = range(0, 8), range(8, 16)


def columns(q):
    return pl.ds(q * WIDE, WIDE)


def place_of(role):
    return (role + SHIFT) % CHIPS


def rows(role):
    return pl.ds(place_of(role) * BLOCK, BLOCK)


def contract_last(left, right):
    return lax.dot_general(
        left, right, (((1,), (1,)), ((), ())), preferred_element_type=jnp.float32
    )


def contract_first(left, right):
    return lax.dot_general(
        left, right, (((0,), (0,)), ((), ())), preferred_element_type=jnp.float32
    )


def kernel(
    inputs, w_in, w_out, cotangent,
    output, input_grad, w_in_grad, w_out_grad,
    tokens, tokens_twin, w_in_v, w_out_v, w_in_twin, w_out_twin, mine, sums, sums_in, units, send_out, recv_out,
    load_sem, own_sem, gather_send, gather_recv, pair_send, pair_recv, swap_send, swap_recv, sum_send, sum_recv,
    unit_send, unit_recv, twin_send, twin_recv, out_send, out_recv,
):
    row, col = lax.axis_index("row"), lax.axis_index("col")
    z, c = row // 2, lax.rem(row, 2)
    twin = (z * 2 + 1 - c, col)

    def along(offset):
        return (lax.rem(z + offset + CHIPS, CHIPS) * 2 + c, col)

    def across(step):
        return (row, lax.rem(col // 4 + step[0], 4) * 4 + lax.rem(lax.rem(col, 4) + step[1], 4))

    def send(src, dst, send_sem, recv_sem, device):
        pltpu.make_async_remote_copy(
            src_ref=src, dst_ref=dst, send_sem=send_sem, recv_sem=recv_sem,
            device_id=device, device_id_type=MESH,
        ).start()

    def wait(ref, sem):
        pltpu.make_async_copy(ref, ref, sem).wait()

    here_at = lax.rem(z - col + SHIFT + CHIPS, CHIPS)
    here = pl.ds(pl.multiple_of(here_at * BLOCK, BLOCK), BLOCK)

    own = [
        pltpu.make_async_copy(source, tokens.at[k, here], own_sem.at[k])
        for k, source in enumerate((inputs, cotangent))
    ]
    loads = [
        pltpu.make_async_copy(w_in.at[:, pl.ds(h * HALF, HALF)], w_in_v.at[h], load_sem.at[h])
        for h in range(2)
    ] + [pltpu.make_async_copy(w_out.at[pl.ds(h * HALF, HALF)], w_out_v.at[h], load_sem.at[2 + h]) for h in range(2)]
    for copy in own + loads:
        copy.start()

    barrier = pltpu.get_barrier_semaphore()
    peers = [across(step) for step in FAR_FIRST[:5]] + [along(offset) for offset in OFFSETS]
    peers += [across(step) for step in FAR_FIRST[5:]] + [twin]
    for peer in peers:
        pl.semaphore_signal(barrier, inc=1, device_id=peer, device_id_type=MESH)
    pl.semaphore_wait(barrier, len(peers))

    for k in range(2):
        own[k].wait()
        for step in FAR_FIRST:
            send(tokens.at[k, here], tokens.at[k, here], gather_send.at[k], gather_recv.at[k], across(step))
        if k == 0:
            theirs = w_in.at[:, pl.ds(pl.multiple_of((1 - c) * HALF, HALF), HALF)]
            send(theirs, w_in_twin, swap_send.at[0], swap_recv.at[0], twin)
        else:
            theirs = w_out.at[pl.ds(pl.multiple_of((1 - c) * HALF, HALF), HALF)]
            send(theirs, w_out_twin, swap_send.at[1], swap_recv.at[1], twin)
    for copy in loads:
        copy.wait()

    def swap_tokens(k):
        wait(tokens.at[k, pl.ds(0, (COLS - 1) * BLOCK)], gather_recv.at[k])
        send(tokens.at[k], tokens_twin.at[k], pair_send.at[k], pair_recv.at[k], twin)

    def width_terms(k):
        for q in range(PARTS):
            if k == 0:
                mine[0, :, columns(q)] = jnp.dot(
                    tokens[0], w_in_v[c, :, columns(q)], preferred_element_type=jnp.float32
                )
            else:
                mine[1, :, columns(q)] = contract_last(tokens[1], w_out_v[c, columns(q)])
        wait((w_in_twin, w_out_twin)[k], swap_recv.at[k])
        wait(tokens_twin.at[k], pair_recv.at[k])
        for q in range(PARTS):
            if k == 0:
                mine[0, :, columns(q)] += jnp.dot(
                    tokens_twin[0], w_in_twin[:, columns(q)], preferred_element_type=jnp.float32
                )
            else:
                mine[1, :, columns(q)] += contract_last(tokens_twin[1], w_out_twin[columns(q)])
            for role in SUM_LEVELS[0]:
                pass_on(k, q, role)

    def collected(k, q, role):
        value = mine[k, rows(role), columns(q)]
        for child in CHILDREN[q].get(role, ()):
            wait(sums_in.at[k, rows(child), columns(q)], sum_recv.at[k, q, place_of(child)])
            value = value + sums_in[k, rows(child), columns(q)].astype(jnp.float32)
        return value

    def pass_on(k, q, role):
        sums[k, rows(role), columns(q)] = collected(k, q, role).astype(jnp.bfloat16)
        send(
            sums.at[k, rows(role), columns(q)], sums_in.at[k, rows(role), columns(q)], sum_send.at[k],
            sum_recv.at[k, q, place_of(role)], along(PARENTS[q][role] - role),
        )

    def hand_out(k, q, role):
        for child in CHILDREN[q].get(role, ()):
            send(
                units.at[k, c, rows(role), columns(q)], units.at[k, c, rows(child), columns(q)], unit_send.at[k],
                unit_recv.at[k, q, place_of(child)], along(child - role),
            )

    def hand_over(k, q, role):
        group = 0 if place_of(role) in NEAR else 1
        part = units.at[k, c, rows(role), columns(q)]
        send(part, part, twin_send.at[k], twin_recv.at[k, group], twin)

    def relay(k, roles):
        for q in range(PARTS):
            for role in roles:
                wait(units.at[k, c, rows(role), columns(q)], unit_recv.at[k, q, place_of(role)])
                hand_out(k, q, role)
            for role in roles:
                hand_over(k, q, role)

    def unit_terms(k, group):
        blocks = (NEAR, FAR)[group]
        span = pl.ds(blocks[0] * BLOCK, len(blocks) * BLOCK)

        def terms(h):
            if k == 0:
                return jnp.dot(units[0, h, span], w_out_v[h], preferred_element_type=jnp.float32)
            return contract_last(units[1, h, span], w_in_v[h])

        value = terms(c)
        wait(units.at[k, 1 - c, span], twin_recv.at[k, group])
        value = value + terms(1 - c)
        send_out[k, span] = value.astype(jnp.bfloat16)
        for step in FAR_FIRST:
            device = across(step)
            p = lax.rem(z - device[1] + SHIFT + CHIPS, CHIPS)

            @pl.when((p >= blocks[0]) & (p <= blocks[-1]))
            def _():
                block = pl.ds(pl.multiple_of(p * BLOCK, BLOCK), BLOCK)
                send(send_out.at[k, block], recv_out.at[k, col], out_send.at[k], out_recv.at[k], device)

        @pl.when((here_at >= blocks[0]) & (here_at <= blocks[-1]))
        def _():
            recv_out[k, col] = send_out[k, here]

    swap_tokens(0)
    width_terms(0)
    swap_tokens(1)
    width_terms(1)
    for level in range(1, 3):
        for k in range(2):
            for q in range(PARTS):
                for role in SUM_LEVELS[level]:
                    pass_on(k, q, role)

    slopes = []
    for q in range(PARTS):
        pre_act = collected(0, q, 0)
        inner = jnp.tanh(gelu_coef * (pre_act + cubic_coef * pre_act * pre_act * pre_act))
        units[0, c, rows(0), columns(q)] = (0.5 * pre_act * (1.0 + inner)).astype(jnp.bfloat16)
        hand_out(0, q, 0)
        hand_over(0, q, 0)
        slopes.append(
            0.5 * (1.0 + inner)
            + 0.5 * pre_act * (1.0 - inner * inner) * gelu_coef * (1.0 + 3.0 * cubic_coef * pre_act * pre_act)
        )
    for q in range(PARTS):
        units[1, c, rows(0), columns(q)] = (collected(1, q, 0) * slopes[q]).astype(jnp.bfloat16)
        hand_out(1, q, 0)
        hand_over(1, q, 0)

    for level in range(2):
        for k in range(2):
            relay(k, UNIT_LEVELS[level])
    unit_terms(0, 0)
    relay(0, UNIT_LEVELS[2])
    unit_terms(1, 0)
    unit_terms(0, 1)
    relay(1, UNIT_LEVELS[2])
    unit_terms(1, 1)
    for h in range(2):
        span = pl.ds(h * HALF, HALF)
        w_out_grad[span] = contract_first(units[0, h], tokens[1]).astype(jnp.bfloat16)
        w_in_grad[:, span] = contract_first(tokens[0], units[1, h]).astype(jnp.bfloat16)
    for k in range(2):
        span = pl.ds(0, (COLS - 1) * BLOCK)
        wait(tokens.at[k, span], gather_send.at[k])
        wait((w_in_twin, w_out_twin)[k], swap_send.at[k])
        wait(tokens_twin.at[k], pair_send.at[k])
        wait(sums.at[k, span], sum_send.at[k])
        wait(units.at[k, 0, span], unit_send.at[k])
        wait(units.at[k, 0], twin_send.at[k])
    for k in range(2):
        wait(recv_out.at[k, pl.ds(0, COLS - 1)], out_recv.at[k])
        value = recv_out[k, 0].astype(jnp.float32)
        for source in range(1, COLS):
            value = value + recv_out[k, source].astype(jnp.float32)
        (output, input_grad)[k][...] = value.astype(jnp.bfloat16)

    for k in range(2):
        wait(send_out.at[k, pl.ds(0, (COLS - 1) * BLOCK)], out_send.at[k])


def place(*refs):
    pairs = list(zip(refs[:2], refs[4:6]))
    for source, target in zip(refs[2:4], refs[6:8]):
        count = source.shape[0] // PIECES
        spans = [pl.ds(i * count, count) for i in range(PIECES)]
        pairs += [(source.at[span], target.at[span]) for span in spans]
    copies = [pltpu.make_async_copy(source, target, refs[8].at[i]) for i, (source, target) in enumerate(pairs)]
    for copy in copies:
        copy.start()
    for copy in copies:
        copy.wait()


def exchange(inputs, w_in, w_out, cotangent):
    bf16, f32 = jnp.bfloat16, jnp.float32
    dma = pltpu.SemaphoreType.DMA
    hbm, vmem = pl.BlockSpec(memory_space=pltpu.HBM), pl.BlockSpec(memory_space=pltpu.VMEM)
    return pl.pallas_call(
        kernel,
        out_shape=(
            pltpu.VMEM((BLOCK, DEPTH), bf16),
            pltpu.VMEM((BLOCK, DEPTH), bf16),
            pltpu.VMEM((DEPTH, UNITS), bf16),
            pltpu.VMEM((UNITS, DEPTH), bf16),
        ),
        in_specs=[hbm] * 4,
        out_specs=(vmem,) * 4,
        scratch_shapes=[
            pltpu.VMEM((2, TOKENS, DEPTH), bf16),
            pltpu.VMEM((2, TOKENS, DEPTH), bf16),
            pltpu.VMEM((2, DEPTH, HALF), bf16),
            pltpu.VMEM((2, HALF, DEPTH), bf16),
            pltpu.VMEM((DEPTH, HALF), bf16),
            pltpu.VMEM((HALF, DEPTH), bf16),
            pltpu.VMEM((2, TOKENS, HALF), f32),
            pltpu.VMEM((2, TOKENS, HALF), bf16),
            pltpu.VMEM((2, TOKENS, HALF), bf16),
            pltpu.VMEM((2, 2, TOKENS, HALF), bf16),
            pltpu.VMEM((2, TOKENS, DEPTH), bf16),
            pltpu.VMEM((2, COLS, BLOCK, DEPTH), bf16),
            dma((4,)), dma((2,)), dma((2,)), dma((2,)), dma((2,)), dma((2,)), dma((2,)), dma((2,)),
            dma((2,)), dma((2, PARTS, 16)), dma((2,)), dma((2, PARTS, 16)), dma((2,)), dma((2, 2)), dma((2,)), dma((2,)),
        ],
        compiler_params=pltpu.CompilerParams(
            collective_id=0, has_side_effects=True, vmem_limit_bytes=VMEM_LIMIT
        ),
        name="feed_forward",
    )(inputs, w_in, w_out, cotangent)


def local(inputs, w_in, w_out, cotangent):
    held = [pltpu.with_memory_space_constraint(array, pltpu.HBM) for array in (inputs, w_in, w_out, cotangent)]
    results = [pltpu.with_memory_space_constraint(array, pltpu.VMEM) for array in exchange(*held)]
    return pl.pallas_call(
        place,
        out_shape=tuple(pltpu.HBM(result.shape, result.dtype) for result in results),
        in_specs=[pl.BlockSpec(memory_space=pltpu.VMEM)] * 4,
        out_specs=(pl.BlockSpec(memory_space=pltpu.HBM),) * 4,
        scratch_shapes=[pltpu.SemaphoreType.DMA((2 + 2 * PIECES,))],
        compiler_params=pltpu.CompilerParams(vmem_limit_bytes=1024 * 1024),
        name="place",
    )(*results)


def solution(mesh):
    placed = (P("col", "row"), P("row", "col"), P("col", "row"), P("col", "row"))
    return jax.shard_map(
        local,
        mesh=mesh,
        in_specs=placed,
        out_specs=(P("col", "row"), P("col", "row"), P("row", "col"), P("col", "row")),
        check_vma=False,
    )
```

```python
import jax
import jax.numpy as jnp
from jax import lax
from jax.experimental import pallas as pl
from jax.experimental.pallas import tpu as pltpu
from jax.sharding import PartitionSpec as P

MESH = pl.DeviceIdType.MESH
gelu_coef = 0.7978845608
cubic_coef = 0.044715

CHIPS = 16
COLS = 16
BLOCK = 16
TOKENS = 256
DEPTH = 384
UNITS = 1536
HALF = 768
PIECES = 4
PARTS = 2
WIDE = HALF // PARTS
VMEM_LIMIT = 32 * 1024 * 1024

SIDES = {
    3: 0, -3: 0, 1: 0, -1: 0, 6: 3, -6: -3, 4: 3, -4: -3, 2: 1, -2: -1, 7: 6, -7: -6, 5: 4, -5: -4,
}
PARENTS = (SIDES | {8: 6}, SIDES | {8: -6})


def children_of(parents):
    children = {}
    for child in sorted(parents, key=lambda role: -abs(role)):
        children.setdefault(parents[child], []).append(child)
    return children


def depth(role, parents):
    return 1 + depth(parents[role], parents) if role else 0


def levels(parents):
    found = {}
    for role in sorted(parents, key=lambda role: -abs(role)):
        found.setdefault(depth(role, parents), []).append(role)
    return [found[level] for level in sorted(found)]


CHILDREN = [children_of(parents) for parents in PARENTS]
UNIT_LEVELS = levels(PARENTS[0])
SUM_LEVELS = UNIT_LEVELS[::-1]
FAR_FIRST = (
    (2, 2), (1, 2), (3, 2), (2, 1), (2, 3), (0, 2), (2, 0), (1, 1), (1, 3), (3, 1), (3, 3), (0, 1), (0, 3), (1, 0), (3, 0),
)
OFFSETS = sorted({(way * (tree[r] - r) + 8) % CHIPS - 8 for tree in PARENTS for r in tree for way in (1, -1)})
SHIFT = 3
NEAR, FAR = range(0, 8), range(8, 16)


def columns(q):
    return pl.ds(q * WIDE, WIDE)


def place_of(role):
    return (role + SHIFT) % CHIPS


def rows(role):
    return pl.ds(place_of(role) * BLOCK, BLOCK)


def contract_last(left, right):
    return lax.dot_general(
        left, right, (((1,), (1,)), ((), ())), preferred_element_type=jnp.float32
    )


def contract_first(left, right):
    return lax.dot_general(
        left, right, (((0,), (0,)), ((), ())), preferred_element_type=jnp.float32
    )


def kernel(
    inputs, w_in, w_out, cotangent,
    output, input_grad, w_in_grad, w_out_grad,
    tokens, tokens_twin, w_in_v, w_out_v, w_in_twin, w_out_twin, mine, sums, sums_in, units, send_out, recv_out,
    load_sem, own_sem, gather_send, gather_recv, pair_send, pair_recv, swap_send, swap_recv, sum_send, sum_recv,
    unit_send, unit_recv, twin_send, twin_recv, out_send, out_recv,
):
    row, col = lax.axis_index("row"), lax.axis_index("col")
    z, c = row // 2, lax.rem(row, 2)
    twin = (z * 2 + 1 - c, col)

    def along(offset):
        return (lax.rem(z + offset + CHIPS, CHIPS) * 2 + c, col)

    def across(step):
        return (row, lax.rem(col // 4 + step[0], 4) * 4 + lax.rem(lax.rem(col, 4) + step[1], 4))

    def send(src, dst, send_sem, recv_sem, device):
        pltpu.make_async_remote_copy(
            src_ref=src, dst_ref=dst, send_sem=send_sem, recv_sem=recv_sem,
            device_id=device, device_id_type=MESH,
        ).start()

    def wait(ref, sem):
        pltpu.make_async_copy(ref, ref, sem).wait()

    here_at = lax.rem(z - col + SHIFT + CHIPS, CHIPS)
    here = pl.ds(pl.multiple_of(here_at * BLOCK, BLOCK), BLOCK)

    own = [
        pltpu.make_async_copy(source, tokens.at[k, here], own_sem.at[k])
        for k, source in enumerate((inputs, cotangent))
    ]
    loads = [
        pltpu.make_async_copy(w_in.at[:, pl.ds(h * HALF, HALF)], w_in_v.at[h], load_sem.at[h])
        for h in range(2)
    ] + [pltpu.make_async_copy(w_out.at[pl.ds(h * HALF, HALF)], w_out_v.at[h], load_sem.at[2 + h]) for h in range(2)]
    barrier = pltpu.get_barrier_semaphore()
    peers = [across(step) for step in FAR_FIRST[:5]] + [along(offset) for offset in OFFSETS]
    peers += [across(step) for step in FAR_FIRST[5:]] + [twin]
    for peer in peers:
        pl.semaphore_signal(barrier, inc=1, device_id=peer, device_id_type=MESH)
    for copy in own + loads:
        copy.start()
    pl.semaphore_wait(barrier, len(peers))

    for k in range(2):
        own[k].wait()
        for step in FAR_FIRST:
            send(tokens.at[k, here], tokens.at[k, here], gather_send.at[k], gather_recv.at[k], across(step))
        if k == 0:
            theirs = w_in.at[:, pl.ds(pl.multiple_of((1 - c) * HALF, HALF), HALF)]
            send(theirs, w_in_twin, swap_send.at[0], swap_recv.at[0], twin)
        else:
            theirs = w_out.at[pl.ds(pl.multiple_of((1 - c) * HALF, HALF), HALF)]
            send(theirs, w_out_twin, swap_send.at[1], swap_recv.at[1], twin)
    for copy in loads:
        copy.wait()

    def swap_tokens(k):
        wait(tokens.at[k, pl.ds(0, (COLS - 1) * BLOCK)], gather_recv.at[k])
        send(tokens.at[k], tokens_twin.at[k], pair_send.at[k], pair_recv.at[k], twin)

    def width_terms(k):
        for q in range(PARTS):
            if k == 0:
                mine[0, :, columns(q)] = jnp.dot(
                    tokens[0], w_in_v[c, :, columns(q)], preferred_element_type=jnp.float32
                )
            else:
                mine[1, :, columns(q)] = contract_last(tokens[1], w_out_v[c, columns(q)])
        wait((w_in_twin, w_out_twin)[k], swap_recv.at[k])
        wait(tokens_twin.at[k], pair_recv.at[k])
        for q in range(PARTS):
            if k == 0:
                mine[0, :, columns(q)] += jnp.dot(
                    tokens_twin[0], w_in_twin[:, columns(q)], preferred_element_type=jnp.float32
                )
            else:
                mine[1, :, columns(q)] += contract_last(tokens_twin[1], w_out_twin[columns(q)])
            for role in SUM_LEVELS[0]:
                pass_on(k, q, role)

    def collected(k, q, role):
        value = mine[k, rows(role), columns(q)]
        for child in CHILDREN[q].get(role, ()):
            wait(sums_in.at[k, rows(child), columns(q)], sum_recv.at[k, q, place_of(child)])
            value = value + sums_in[k, rows(child), columns(q)].astype(jnp.float32)
        return value

    def pass_on(k, q, role):
        sums[k, rows(role), columns(q)] = collected(k, q, role).astype(jnp.bfloat16)
        send(
            sums.at[k, rows(role), columns(q)], sums_in.at[k, rows(role), columns(q)], sum_send.at[k],
            sum_recv.at[k, q, place_of(role)], along(PARENTS[q][role] - role),
        )

    def hand_out(k, q, role):
        for child in CHILDREN[q].get(role, ()):
            send(
                units.at[k, c, rows(role), columns(q)], units.at[k, c, rows(child), columns(q)], unit_send.at[k],
                unit_recv.at[k, q, place_of(child)], along(child - role),
            )

    def hand_over(k, q, role):
        group = 0 if place_of(role) in NEAR else 1
        part = units.at[k, c, rows(role), columns(q)]
        send(part, part, twin_send.at[k], twin_recv.at[k, group], twin)

    def relay(k, roles):
        for q in range(PARTS):
            for role in roles:
                wait(units.at[k, c, rows(role), columns(q)], unit_recv.at[k, q, place_of(role)])
                hand_out(k, q, role)
                if role not in CHILDREN[q]:
                    hand_over(k, q, role)
            for role in roles:
                if role in CHILDREN[q]:
                    hand_over(k, q, role)

    def unit_terms(k, group):
        blocks = (NEAR, FAR)[group]
        span = pl.ds(blocks[0] * BLOCK, len(blocks) * BLOCK)

        def terms(h):
            if k == 0:
                return jnp.dot(units[0, h, span], w_out_v[h], preferred_element_type=jnp.float32)
            return contract_last(units[1, h, span], w_in_v[h])

        value = terms(c)
        wait(units.at[k, 1 - c, span], twin_recv.at[k, group])
        value = value + terms(1 - c)
        send_out[k, span] = value.astype(jnp.bfloat16)
        for step in FAR_FIRST:
            device = across(step)
            p = lax.rem(z - device[1] + SHIFT + CHIPS, CHIPS)

            @pl.when((p >= blocks[0]) & (p <= blocks[-1]))
            def _():
                block = pl.ds(pl.multiple_of(p * BLOCK, BLOCK), BLOCK)
                send(send_out.at[k, block], recv_out.at[k, col], out_send.at[k], out_recv.at[k], device)

        @pl.when((here_at >= blocks[0]) & (here_at <= blocks[-1]))
        def _():
            recv_out[k, col] = send_out[k, here]

    swap_tokens(0)
    width_terms(0)
    swap_tokens(1)
    width_terms(1)
    for level in range(1, 3):
        for k in range(2):
            for q in range(PARTS):
                for role in SUM_LEVELS[level]:
                    pass_on(k, q, role)

    slopes = []
    for q in range(PARTS):
        pre_act = collected(0, q, 0)
        inner = jnp.tanh(gelu_coef * (pre_act + cubic_coef * pre_act * pre_act * pre_act))
        units[0, c, rows(0), columns(q)] = (0.5 * pre_act * (1.0 + inner)).astype(jnp.bfloat16)
        hand_out(0, q, 0)
        hand_over(0, q, 0)
        slopes.append(
            0.5 * (1.0 + inner)
            + 0.5 * pre_act * (1.0 - inner * inner) * gelu_coef * (1.0 + 3.0 * cubic_coef * pre_act * pre_act)
        )
    for q in range(PARTS):
        units[1, c, rows(0), columns(q)] = (collected(1, q, 0) * slopes[q]).astype(jnp.bfloat16)
        hand_out(1, q, 0)
        hand_over(1, q, 0)

    for level in range(2):
        for k in range(2):
            relay(k, UNIT_LEVELS[level])
    unit_terms(0, 0)
    relay(0, UNIT_LEVELS[2])
    unit_terms(1, 0)
    unit_terms(0, 1)
    relay(1, UNIT_LEVELS[2])
    unit_terms(1, 1)
    for h in range(2):
        span = pl.ds(h * HALF, HALF)
        w_out_grad[span] = contract_first(units[0, h], tokens[1]).astype(jnp.bfloat16)
        w_in_grad[:, span] = contract_first(tokens[0], units[1, h]).astype(jnp.bfloat16)
    for k in range(2):
        span = pl.ds(0, (COLS - 1) * BLOCK)
        wait(tokens.at[k, span], gather_send.at[k])
        wait((w_in_twin, w_out_twin)[k], swap_send.at[k])
        wait(tokens_twin.at[k], pair_send.at[k])
        wait(sums.at[k, span], sum_send.at[k])
        wait(units.at[k, 0, span], unit_send.at[k])
        wait(units.at[k, 0], twin_send.at[k])
    for k in range(2):
        wait(recv_out.at[k, pl.ds(0, COLS - 1)], out_recv.at[k])
        value = recv_out[k, 0].astype(jnp.float32)
        for source in range(1, COLS):
            value = value + recv_out[k, source].astype(jnp.float32)
        (output, input_grad)[k][...] = value.astype(jnp.bfloat16)

    for k in range(2):
        wait(send_out.at[k, pl.ds(0, (COLS - 1) * BLOCK)], out_send.at[k])


def place(*refs):
    pairs = list(zip(refs[:2], refs[4:6]))
    for source, target in zip(refs[2:4], refs[6:8]):
        count = source.shape[0] // PIECES
        spans = [pl.ds(i * count, count) for i in range(PIECES)]
        pairs += [(source.at[span], target.at[span]) for span in spans]
    copies = [pltpu.make_async_copy(source, target, refs[8].at[i]) for i, (source, target) in enumerate(pairs)]
    for copy in copies:
        copy.start()
    for copy in copies:
        copy.wait()


def exchange(inputs, w_in, w_out, cotangent):
    bf16, f32 = jnp.bfloat16, jnp.float32
    dma = pltpu.SemaphoreType.DMA
    hbm, vmem = pl.BlockSpec(memory_space=pltpu.HBM), pl.BlockSpec(memory_space=pltpu.VMEM)
    return pl.pallas_call(
        kernel,
        out_shape=(
            pltpu.VMEM((BLOCK, DEPTH), bf16),
            pltpu.VMEM((BLOCK, DEPTH), bf16),
            pltpu.VMEM((DEPTH, UNITS), bf16),
            pltpu.VMEM((UNITS, DEPTH), bf16),
        ),
        in_specs=[hbm] * 4,
        out_specs=(vmem,) * 4,
        scratch_shapes=[
            pltpu.VMEM((2, TOKENS, DEPTH), bf16),
            pltpu.VMEM((2, TOKENS, DEPTH), bf16),
            pltpu.VMEM((2, DEPTH, HALF), bf16),
            pltpu.VMEM((2, HALF, DEPTH), bf16),
            pltpu.VMEM((DEPTH, HALF), bf16),
            pltpu.VMEM((HALF, DEPTH), bf16),
            pltpu.VMEM((2, TOKENS, HALF), f32),
            pltpu.VMEM((2, TOKENS, HALF), bf16),
            pltpu.VMEM((2, TOKENS, HALF), bf16),
            pltpu.VMEM((2, 2, TOKENS, HALF), bf16),
            pltpu.VMEM((2, TOKENS, DEPTH), bf16),
            pltpu.VMEM((2, COLS, BLOCK, DEPTH), bf16),
            dma((4,)), dma((2,)), dma((2,)), dma((2,)), dma((2,)), dma((2,)), dma((2,)), dma((2,)),
            dma((2,)), dma((2, PARTS, 16)), dma((2,)), dma((2, PARTS, 16)), dma((2,)), dma((2, 2)), dma((2,)), dma((2,)),
        ],
        compiler_params=pltpu.CompilerParams(
            collective_id=0, has_side_effects=True, vmem_limit_bytes=VMEM_LIMIT
        ),
        name="feed_forward",
    )(inputs, w_in, w_out, cotangent)


def local(inputs, w_in, w_out, cotangent):
    held = [pltpu.with_memory_space_constraint(array, pltpu.HBM) for array in (inputs, w_in, w_out, cotangent)]
    results = [pltpu.with_memory_space_constraint(array, pltpu.VMEM) for array in exchange(*held)]
    return pl.pallas_call(
        place,
        out_shape=tuple(pltpu.HBM(result.shape, result.dtype) for result in results),
        in_specs=[pl.BlockSpec(memory_space=pltpu.VMEM)] * 4,
        out_specs=(pl.BlockSpec(memory_space=pltpu.HBM),) * 4,
        scratch_shapes=[pltpu.SemaphoreType.DMA((2 + 2 * PIECES,))],
        compiler_params=pltpu.CompilerParams(vmem_limit_bytes=1024 * 1024),
        name="place",
    )(*results)


def solution(mesh):
    placed = (P("col", "row"), P("row", "col"), P("col", "row"), P("col", "row"))
    return jax.shard_map(
        local,
        mesh=mesh,
        in_specs=placed,
        out_specs=(P("col", "row"), P("col", "row"), P("row", "col"), P("col", "row")),
        check_vma=False,
    )
```
